128 devices in a mesh: student: 4 (over x_lo, core), ctx: 32 (over x_hi, z, y).
Axes of the slice: x: 4 (x_hi: 2, x_lo: 2; x = x_hi * 2 + x_lo), y: 4, z: 4, core: 2. Of those that a mesh axis runs over, the one named last changes fastest.
Arguments:
- query_states: bfloat16 [4, 8192, 2048], P('student', 'ctx'), may hold values from -30 to 30
- key_states: bfloat16 [4, 8192, 512], P('student', 'ctx'), may hold values from -7 to 7
- value_states: bfloat16 [4, 8192, 512], P('student', 'ctx'), may hold values from -6 to 6
- layer_inputs: bfloat16 [4, 8192, 2048], P('student', 'ctx'), may hold values from -6 to 6
- out_weight: bfloat16 [4, 2048, 2048], P('student'), may hold values from -0.5 to 0.5
- teacher: bfloat16 [8192, 8192], P('ctx', 'student'), may hold values from -6 to 6
- teacher_map: bfloat16 [8192, 2048], P('student'), may hold values from -0.0625 to 0.0625
- offsets: int32 [64], replicated, may hold values from 0 to 8064, as said below
Outputs:
- student_hidden: bfloat16 [4, 8192, 2048], P('student', 'ctx')
- weight_grad: float32 [4, 2048, 2048], P('student', 'ctx')
The draws below stay inside these ranges and needn't reach their ends.
Inputs may be any that keep to these rules, and one draw needn't show every extreme that they name: offsets is a permutation of the 64 values 0, 128, 256, ..., 8064.
All inputs are finite; a program needn't handle non-finite values.
Results may differ from the reference program's by a relative error of at most 0.0037.
Values may be sent and summed in bfloat16 or wider, within the bound.
A program may use at most 128 MiB of HBM per device.

```python
import jax
import jax.numpy as jnp
from jax import lax

D = 2048
HQ = 16
HK = 4
HD = 128
TW = 8192
TOK_DEV = 256
HQD = 2048
BLK = 128
BLOCKS = 64
TOKENS = 8192
STUDENTS = 4


def paired_states(key):
    key_query = jax.random.fold_in(key, 11)
    key_key = jax.random.fold_in(key, 12)
    shape_query = (STUDENTS, TOKENS, HQ * HD)
    shape_key = (STUDENTS, TOKENS, HK * HD)
    query_out = 1.4 * jax.random.truncated_normal(key_query, -4.5, 4.5, shape_query, jnp.float32)
    key_out = 1.4 * jax.random.truncated_normal(key_key, -4.5, 4.5, shape_key, jnp.float32)
    return (query_out, key_out)


def draw_query_states(key, part):
    return paired_states(key)[0].astype(jnp.bfloat16)


def draw_key_states(key, part):
    return paired_states(key)[1].astype(jnp.bfloat16)


def draw_offsets(key, part):
    order = jax.random.permutation(jax.random.fold_in(key, 13), BLOCKS)
    return (order * BLK).astype(jnp.int32)


def block_scale(rng, dims, split, least, high):
    loudness = 1.0
    for dim, parts in split:
        draws = jax.random.uniform(jax.random.fold_in(jax.random.fold_in(rng, 6), dim), (parts,), jnp.float32, least / len(split), high / len(split))
        loudness = loudness * jnp.repeat(jnp.exp(draws), dims[dim] // parts).reshape((-1,) + (1,) * (len(dims) - 1 - dim))
    return loudness


def normal_values(rng, shape, deviation, limit, split=(), kind=jnp.bfloat16):
    result = jax.random.normal(rng, shape, jnp.float32) * deviation
    if len(split) > 0:
        result = block_scale(rng, shape, split, -0.22, 0.18) * result
    return jnp.clip(result, min=-limit, max=limit).astype(kind)


def setup_inputs(seed: int = 0) -> dict:
    streams_of = jax.random.split(jax.random.key(seed), 9)
    return {
        "query_states": draw_query_states(jax.random.fold_in(streams_of[8], 71), 0),
        "key_states": draw_key_states(jax.random.fold_in(streams_of[8], 71), 0),
        "value_states": normal_values(streams_of[2], (STUDENTS, TOKENS, HK * HD), 1.0, 6.0, ((0, 4), (1, 32))),
        "layer_inputs": normal_values(streams_of[3], (STUDENTS, TOKENS, D), 1.0, 6.0, ((0, 4), (1, 32))),
        "out_weight": normal_values(streams_of[4], (STUDENTS, HQD, D), (HQD // 16) ** -0.5, 0.5, ((0, 4),)),
        "teacher": normal_values(streams_of[5], (TOKENS, TW), 1.0, 6.0, ((0, 32), (1, 4))),
        "teacher_map": normal_values(streams_of[6], (TW, D), TW ** -0.5, 0.0625, ((0, 4),)),
        "offsets": draw_offsets(jax.random.fold_in(streams_of[8], 71), 0),
    }


def reference(query_states, key_states, value_states, layer_inputs, out_weight, teacher, teacher_map, offsets):
    row_ids = jnp.arange(TOKENS, dtype=jnp.int32)
    position = offsets[row_ids // BLK] + row_ids % BLK
    target = jnp.dot(teacher, teacher_map, preferred_element_type=jnp.float32)
    group = HQ // HK
    scale_att = HD ** (-0.5)
    scale_err = 1.0 / jnp.sqrt(jnp.float32(TOKENS))
    hidden_list = []
    grad_list = []
    for student in range(STUDENTS):
        key_all = key_states[student].reshape(TOKENS, HK, HD).astype(jnp.float32)
        value_all = value_states[student].reshape(TOKENS, HK, HD).astype(jnp.float32)
        query_blocks = query_states[student].reshape(TOKENS // TOK_DEV, TOK_DEV, HK, group, HD)
        pos_blocks = position.reshape(TOKENS // TOK_DEV, TOK_DEV)

        def attend(pair):
            query_block, query_pos = pair
            scores = jnp.einsum('qhgd,khd->hgqk', query_block.astype(jnp.float32), key_all) * scale_att
            allowed = position[None, :] <= query_pos[:, None]
            masked = jnp.where(allowed[None, None], scores, -jnp.inf)
            row_max = lax.optimization_barrier(jnp.max(masked, axis=-1, keepdims=True))
            expo = jnp.where(allowed[None, None], jnp.exp(scores - row_max), 0.0)
            total = lax.optimization_barrier(jnp.sum(expo, axis=-1))
            summed = jnp.einsum('hgqk,khd->qhgd', expo, value_all, precision=lax.Precision.HIGHEST)
            normed = summed / jnp.transpose(total, (2, 0, 1))[..., None]
            return normed.reshape(TOK_DEV, HQD).astype(jnp.bfloat16)
        attended = lax.map(attend, (query_blocks, pos_blocks)).reshape(TOKENS, HQD)
        student_f32 = layer_inputs[student].astype(jnp.float32) + jnp.dot(attended, out_weight[student], preferred_element_type=jnp.float32)
        hidden_list.append(student_f32.astype(jnp.bfloat16))
        match_grad = ((student_f32 - target) * scale_err).astype(jnp.bfloat16)
        grad_list.append(jnp.dot(attended.T, match_grad, preferred_element_type=jnp.float32))
    return (jnp.stack(hidden_list), jnp.stack(grad_list))
```

```python
import math

import jax
import jax.numpy as jnp
from jax import lax
from jax.experimental import pallas as pl
from jax.experimental.pallas import tpu as pltpu
from jax.sharding import PartitionSpec as P

F32 = jnp.float32
BF16 = jnp.bfloat16
N = 32
HD = 128
SCALE = HD**-0.5 * math.log2(math.e)
ERR = 1.0 / math.sqrt(8192.0)
NEG = -1e30
GROUPS = 8
M = 512
CW = 1024
MESH = pl.DeviceIdType.MESH


def kernel(
    q, k, v, li, w, te, tm, order,
    sh_out, wg_out,
    li_v, w_v, te_v, tm_v, kv, q_recv, qp, kpos, vp, att, d_home, d_recv, dpos,
    tp, tx, tt, th, th_recv, mg, aw, sh_send, sh_recv, wg_send, wg_recv,
    sa, sb, m_ref, acc,
    loc, loc_tm, s1_s, s1_r, g_s, g_r, x_s, x_r, q_s, q_r, t_s, t_r, d_s, d_r,
    ag_s, ag_r, sh_s, sh_r, wg_s, wg_r,
):
    stu = lax.axis_index("student")
    me = lax.axis_index("ctx")
    core = lax.rem(stu, 2)
    xlo = stu // 2
    xh = me // 16
    mid, low = lax.rem(me // 4, 4), lax.rem(me, 4)
    a = jnp.where(core == 0, low, mid)
    b = jnp.where(core == 0, mid, low)
    t = xh * 4 + b
    mine = xh * 16 + b * 4 + a

    def ctx_of(x_, a_, b_):
        return x_ * 16 + jnp.where(core == 0, b_ * 4 + a_, a_ * 4 + b_)

    def remote(src, dst, ss, rs, where):
        return pltpu.make_async_remote_copy(
            src_ref=src, dst_ref=dst, send_sem=ss, recv_sem=rs, device_id=where, device_id_type=MESH
        )

    def cols(i, width):
        return pl.ds(pl.multiple_of(i * width, width), width)

    def peer(kk, sign):
        dx, db, da = kk // 16, lax.rem(kk // 4, 4), lax.rem(kk, 4)
        x_ = lax.rem(xh + dx, 2)
        a_ = lax.rem(a + sign * da + 4, 4)
        b_ = lax.rem(b + sign * db + 4, 4)
        return x_, a_, b_

    tm_loads = [
        pltpu.make_async_copy(tm.at[:, pl.ds(512 * i, 512)], tm_v.at[i % 2], loc_tm.at[i % 2])
        for i in range(4)
    ]
    c_te = pltpu.make_async_copy(te, te_v, loc.at[0])
    c_li = pltpu.make_async_copy(li, li_v, loc.at[1])
    c_w = pltpu.make_async_copy(w.at[:, cols(a, 512)], w_v, loc.at[2])
    c_k = pltpu.make_async_copy(k.at[:, :, cols(a, HD)], kv.at[mine, 0], loc.at[3])
    c_v = pltpu.make_async_copy(v.at[:, :, cols(a, HD)], kv.at[mine, 1], loc.at[4])
    c_q = pltpu.make_async_copy(q.at[:, cols(t, 16), cols(a, 512)], q_recv.at[mine], loc.at[5])
    for c in (c_k, c_v, c_q, c_te, tm_loads[0], tm_loads[1], c_li, c_w):
        c.start()

    barrier = pltpu.get_barrier_semaphore()

    def greet(i, _):
        pl.semaphore_signal(barrier, inc=1, device_id={"ctx": lax.rem(me + i, N)}, device_id_type=MESH)
        return 0

    lax.fori_loop(1, N, greet, 0)
    pair_core = {"student": xlo * 2 + 1 - core}
    pair_xlo = {"student": (1 - xlo) * 2 + core}
    pl.semaphore_signal(barrier, inc=1, device_id=pair_core, device_id_type=MESH)
    pl.semaphore_signal(barrier, inc=1, device_id=pair_xlo, device_id_type=MESH)
    pl.semaphore_wait(barrier, N + 1)

    firsts = []
    for da in range(1, 4):
        to = lax.rem(a + da, 4)
        for i, src in enumerate((k, v)):
            firsts.append(
                remote(
                    src.at[:, :, cols(to, HD)], kv.at[mine, i], s1_s.at[da, i], s1_r.at[da, i],
                    {"ctx": ctx_of(xh, to, b)},
                )
            )
    for c in firsts:
        c.start()

    def q_copy(kk, sign=1):
        x_, a_, b_ = peer(kk, sign)
        return remote(
            q.at[:, cols(x_ * 4 + b_, 16), cols(a_, 512)], q_recv.at[mine], q_s.at[kk], q_r.at[kk],
            {"ctx": ctx_of(x_, a_, b_)},
        )

    def q_start(kk, _):
        q_copy(kk).start()
        return 0

    lax.fori_loop(1, N, q_start, 0)
    c_k.wait()
    c_v.wait()
    for da in range(1, 4):
        frm = lax.rem(a - da + 4, 4)
        for i in range(2):
            at = kv.at[xh * 16 + b * 4 + frm, i]
            remote(at, at, s1_s.at[da, i], s1_r.at[da, i], {"ctx": ctx_of(xh, frm, b)}).wait_recv()
    own = kv.at[pl.ds(xh * 16 + b * 4, 4)]
    other = kv.at[pl.ds((1 - xh) * 16 + b * 4, 4)]
    seconds = [remote(own, own, g_s.at[0], g_r.at[0], {"ctx": ctx_of(1 - xh, a, b)})]
    for db in range(1, 4):
        seconds.append(
            remote(own, own, g_s.at[db], g_r.at[db], {"ctx": ctx_of(xh, a, lax.rem(b + db, 4))})
        )
    for c in seconds:
        c.start()

    vp[:, HD:] = jnp.ones((8192, HD), BF16)
    c_te.wait()
    for i in range(4):
        tm_loads[i].wait()
        tp[:, 512 * i : 512 * i + 512] = jnp.dot(te_v[...], tm_v[i % 2], preferred_element_type=F32)
        if i < 2:
            tm_loads[i + 2].start()
    half = pl.ds(pl.multiple_of(core * 128, 128), 128)
    half2 = pl.ds(pl.multiple_of((1 - core) * 128, 128), 128)
    t1 = remote(tp.at[half2], tx, t_s.at[0], t_r.at[0], pair_core)
    t1.start()
    t1.wait()
    th[...] = (tp[half, :] + tx[...]).astype(BF16)
    t2 = remote(th, th_recv, t_s.at[1], t_r.at[1], pair_xlo)
    t2.start()

    remote(other, other, g_s.at[0], g_r.at[0], {"ctx": ctx_of(1 - xh, a, b)}).wait_recv()
    thirds = []
    for db in range(1, 4):
        thirds.append(
            remote(other, other, x_s.at[db], x_r.at[db], {"ctx": ctx_of(xh, a, lax.rem(b + db, 4))})
        )
    for c in thirds:
        c.start()
    t2.wait()
    tp[half, :] = tp[half, :] + tx[...] + th_recv[...].astype(F32)
    t3 = remote(tp.at[half], tt, t_s.at[2], t_r.at[2], pair_core)
    t3.start()
    c_li.wait()
    d_home[core] = (li_v[core].astype(F32) - tp[half, :]).astype(BF16)
    t3.wait()
    d_home[1 - core] = (li_v[1 - core].astype(F32) - tt[...]).astype(BF16)

    c_q.wait()

    def q_wait(kk, _):
        x_, a_, b_ = peer(kk, -1)
        at = q_recv.at[x_ * 16 + b_ * 4 + a_]
        remote(at, at, q_s.at[kk], q_r.at[kk], {"ctx": ctx_of(x_, a_, b_)}).wait_recv()
        return 0

    lax.fori_loop(1, N, q_wait, 0)
    for db in range(1, 4):
        frm = lax.rem(b - db + 4, 4)
        at = kv.at[pl.ds(xh * 16 + frm * 4, 4)]
        remote(at, at, g_s.at[db], g_r.at[db], {"ctx": ctx_of(xh, a, frm)}).wait_recv()
        at = kv.at[pl.ds((1 - xh) * 16 + frm * 4, 4)]
        remote(at, at, x_s.at[db], x_r.at[db], {"ctx": ctx_of(xh, a, frm)}).wait_recv()

    def d_copy(kk):
        x_, a_, b_ = peer(kk, 1)
        return remote(
            d_home.at[:, cols(x_ * 4 + b_, 16), cols(a_, 512)], d_recv.at[mine], d_s.at[kk], d_r.at[kk],
            {"ctx": ctx_of(x_, a_, b_)},
        )

    def d_start(kk, _):
        d_copy(kk).start()
        return 0

    lax.fori_loop(1, N, d_start, 0)
    d_recv[mine] = d_home[:, cols(t, 16), cols(a, 512)]

    def arrange(p, _):
        at = order[64 + p]
        part = order[128 + p]
        to = pl.ds(pl.multiple_of(p * 128, 128), 128)
        kpos[to, :] = kv[at, 0, part]
        vp[to, :HD] = kv[at, 1, part]
        slab = q_recv[at, part]
        for h in range(4):
            qp[p // 8, h, pl.ds(pl.multiple_of(lax.rem(p, 8) * 16, 16), 16), :] = slab[:, h * HD : h * HD + HD]
        return 0

    lax.fori_loop(0, 64, arrange, 0)

    def score(g, j, dst):
        dst[...] = lax.dot_general(
            qp[g].reshape(M, HD), kpos[cols(j, CW), :], (((1,), (1,)), ((), ())), preferred_element_type=F32
        )

    def absorb(src, j, diagonal=False):
        s = src[...]
        if diagonal:
            row = lax.rem(lax.broadcasted_iota(jnp.int32, (M, CW), 0), 128)
            col = lax.broadcasted_iota(jnp.int32, (M, CW), 1)
            s = jnp.where(col <= (row // 16) * 128 + t * 16 + lax.rem(row, 16), s, NEG)
        old = m_ref[...]
        new = jnp.maximum(old, jnp.max(s, axis=1, keepdims=True))
        m_ref[...] = new
        factor = jnp.exp2((old - new) * SCALE)
        p = jnp.exp2(s * SCALE - jnp.tile(new * SCALE, (1, CW // 128))).astype(BF16)
        acc[...] = acc[...] * jnp.tile(factor, (1, 2)) + jnp.dot(
            p, vp[cols(j, CW), :], preferred_element_type=F32
        )

    def begin():
        m_ref[...] = jnp.full((M, 128), NEG, F32)
        acc[...] = jnp.zeros((M, 256), F32)

    def att_copy(g, da):
        at = att.at[cols(g, 128), cols(a, 512)]
        return remote(at, at, ag_s.at[g, da], ag_r.at[g, da], {"ctx": ctx_of(xh, lax.rem(a + da, 4), b)})

    def finish(g):
        for h in range(4):
            rows = slice(h * 128, h * 128 + 128)
            att[cols(g, 128), pl.ds(pl.multiple_of(a * 512 + h * 128, 128), 128)] = (
                acc[rows, :HD] / acc[rows, HD:]
            ).astype(BF16)
        for da in range(1, 4):
            att_copy(g, da).start()

    def two_groups(u, _):
        g = 2 * u
        begin()
        score(g, 0, sa)

        def even(i, _):
            score(g, 2 * i + 1, sb)
            absorb(sa, 2 * i)
            score(g, 2 * i + 2, sa)
            absorb(sb, 2 * i + 1)
            return 0

        lax.fori_loop(0, u, even, 0)
        score(g + 1, 0, sb)
        absorb(sa, g, True)
        finish(g)
        begin()

        def odd(i, _):
            score(g + 1, 2 * i + 1, sa)
            absorb(sb, 2 * i)
            score(g + 1, 2 * i + 2, sb)
            absorb(sa, 2 * i + 1)
            return 0

        lax.fori_loop(0, u, odd, 0)
        score(g + 1, g + 1, sa)
        absorb(sb, g)
        absorb(sa, g + 1, True)
        finish(g + 1)
        return 0

    lax.fori_loop(0, GROUPS // 2, two_groups, 0)

    def d_wait(kk, _):
        x_, a_, b_ = peer(kk, -1)
        at = d_recv.at[x_ * 16 + b_ * 4 + a_]
        remote(at, at, d_s.at[kk], d_r.at[kk], {"ctx": ctx_of(x_, a_, b_)}).wait_recv()
        return 0

    lax.fori_loop(1, N, d_wait, 0)

    def arrange_d(p, _):
        dpos[cols(p, 16), :] = d_recv[order[64 + p], order[128 + p]]
        return 0

    lax.fori_loop(0, 64, arrange_d, 0)
    c_w.wait()

    def project(i, _):
        for g2 in range(2):
            g = 2 * i + g2
            for da in range(1, 4):
                frm = lax.rem(a - da + 4, 4)
                at = att.at[cols(g, 128), cols(frm, 512)]
                remote(at, at, ag_s.at[g, da], ag_r.at[g, da], {"ctx": ctx_of(xh, frm, b)}).wait_recv()
        rows = cols(i, 256)
        x = jnp.dot(att[rows, :], w_v[...], preferred_element_type=F32)
        aw[pl.ds(16 * i, 16)] = x.astype(BF16).reshape(16, 16, 512)
        mg[rows, :] = ((x + dpos[rows, :].astype(F32)) * ERR).astype(BF16)
        return 0

    lax.fori_loop(0, 4, project, 0)

    def arrange_sh(blk, _):
        sh_send[blk // 2, lax.rem(blk, 2)] = aw[order[blk]]
        return 0

    lax.fori_loop(0, 64, arrange_sh, 0)

    def sh_copy(kk):
        x_, a_, b_ = peer(kk, 1)
        to = ctx_of(x_, a_, b_)
        return remote(
            sh_send.at[to], sh_recv.at[:, cols(t, 16), cols(a, 512)], sh_s.at[kk], sh_r.at[kk], {"ctx": to}
        )

    def sh_start(kk, _):
        sh_copy(kk).start()
        return 0

    lax.fori_loop(1, N, sh_start, 0)
    sh_recv[:, cols(t, 16), cols(a, 512)] = sh_send[me]

    def wg_copy(to):
        return remote(
            wg_send.at[to], wg_recv.at[t, :, cols(a, 512)], wg_s.at[to], wg_r.at[me], {"ctx": to}
        )

    def wgrad(i, _):
        quad = lax.rem(me // 4 + i, 8)
        part = lax.dot_general(
            att[:, cols(quad, 256)], mg[...], (((0,), (0,)), ((), ())), preferred_element_type=F32
        ).astype(BF16)
        wg_send[pl.ds(quad * 4, 4)] = part.reshape(4, 64, 512)
        for r in range(4):
            to = quad * 4 + r

            @pl.when(to != me)
            def _():
                wg_copy(to).start()

        return 0

    lax.fori_loop(0, 8, wgrad, 0)
    wg_recv[t, :, cols(a, 512)] = wg_send[me]

    def sh_wait(kk, _):
        x_, a_, b_ = peer(kk, -1)
        at = sh_recv.at[:, cols(x_ * 4 + b_, 16), cols(a_, 512)]
        remote(sh_send.at[0], at, sh_s.at[kk], sh_r.at[kk], {"ctx": ctx_of(x_, a_, b_)}).wait_recv()
        return 0

    lax.fori_loop(1, N, sh_wait, 0)
    sh_out[...] = (li_v[...].astype(F32) + sh_recv[...].astype(F32)).astype(BF16)

    def wg_wait(kk, _):
        x_, a_, b_ = peer(kk, -1)
        frm = ctx_of(x_, a_, b_)
        at = wg_recv.at[x_ * 4 + b_, :, cols(a_, 512)]
        remote(wg_send.at[0], at, wg_s.at[frm], wg_r.at[frm], {"ctx": frm}).wait_recv()
        return 0

    lax.fori_loop(1, N, wg_wait, 0)
    total = wg_recv[0].astype(F32)
    for i in range(1, 8):
        total = total + wg_recv[i].astype(F32)
    wg_out[...] = total

    for c in firsts + seconds + thirds:
        c.wait_send()

    def drain(kk, _):
        q_copy(kk).wait_send()
        d_copy(kk).wait_send()
        sh_copy(kk).wait_send()
        wg_copy(lax.rem(me + kk, N)).wait_send()
        return 0

    lax.fori_loop(1, N, drain, 0)

    def drain_att(g, _):
        for da in range(1, 4):
            att_copy(g, da).wait_send()
        return 0

    lax.fori_loop(0, GROUPS, drain_att, 0)


def local(query_states, key_states, value_states, layer_inputs, out_weight, teacher, teacher_map, offsets):
    pos = offsets // 128
    ids = jnp.arange(64, dtype=jnp.int32)
    inv = jnp.sum(jnp.where(pos[None, :] == ids[:, None], ids[None, :], 0), axis=1)
    home = inv // 2
    swapped = (home // 16) * 16 + (home % 4) * 4 + (home // 4) % 4
    slot = jnp.where(lax.axis_index("student") % 2 == 0, home, swapped)
    order = jnp.concatenate([pos, slot, inv % 2])
    hbm = pl.BlockSpec(memory_space=pl.ANY)
    vmem = pl.BlockSpec(memory_space=pltpu.VMEM)
    dma = pltpu.SemaphoreType.DMA
    sh, wg = pl.pallas_call(
        kernel,
        name="layer",
        out_shape=(
            jax.ShapeDtypeStruct((2, 128, 2048), BF16),
            jax.ShapeDtypeStruct((64, 2048), F32),
        ),
        in_specs=[hbm] * 7 + [pl.BlockSpec(memory_space=pltpu.SMEM)],
        out_specs=(vmem, vmem),
        scratch_shapes=[
            pltpu.VMEM((2, 128, 2048), BF16),
            pltpu.VMEM((2048, 512), BF16),
            pltpu.VMEM((256, 2048), BF16),
            pltpu.VMEM((2, 2048, 512), BF16),
            pltpu.VMEM((32, 2, 2, 128, 128), BF16),
            pltpu.VMEM((32, 2, 16, 512), BF16),
            pltpu.VMEM((GROUPS, 4, 128, 128), BF16),
            pltpu.VMEM((8192, 128), BF16),
            pltpu.VMEM((8192, 256), BF16),
            pltpu.VMEM((1024, 2048), BF16),
            pltpu.VMEM((2, 128, 2048), BF16),
            pltpu.VMEM((32, 2, 16, 512), BF16),
            pltpu.VMEM((1024, 512), BF16),
            pltpu.VMEM((256, 2048), F32),
            pltpu.VMEM((128, 2048), F32),
            pltpu.VMEM((128, 2048), F32),
            pltpu.VMEM((128, 2048), BF16),
            pltpu.VMEM((128, 2048), BF16),
            pltpu.VMEM((1024, 512), BF16),
            pltpu.VMEM((64, 16, 512), BF16),
            pltpu.VMEM((32, 2, 16, 512), BF16),
            pltpu.VMEM((2, 128, 2048), BF16),
            pltpu.VMEM((32, 64, 512), BF16),
            pltpu.VMEM((8, 64, 2048), BF16),
            pltpu.VMEM((M, CW), F32),
            pltpu.VMEM((M, CW), F32),
            pltpu.VMEM((M, 128), F32),
            pltpu.VMEM((M, 256), F32),
            dma((6,)), dma((2,)),
            dma((4, 2)), dma((4, 2)),
            dma((4,)), dma((4,)), dma((4,)), dma((4,)),
            dma((N,)), dma((N,)), dma((3,)), dma((3,)), dma((N,)), dma((N,)),
            dma((GROUPS, 4)), dma((GROUPS, 4)),
            dma((N,)), dma((N,)), dma((N,)), dma((N,)),
        ],
        compiler_params=pltpu.CompilerParams(
            collective_id=0, has_side_effects=True, vmem_limit_bytes=60 * 1024 * 1024
        ),
    )(
        query_states[0].reshape(2, 128, 2048), key_states[0].reshape(2, 128, 512), value_states[0].reshape(2, 128, 512),
        layer_inputs[0].reshape(2, 128, 2048), out_weight[0], teacher, teacher_map, order,
    )
    return sh.reshape(1, 256, 2048), wg[None]


def solution(mesh):
    return jax.shard_map(
        local,
        mesh=mesh,
        in_specs=(
            P("student", "ctx", None),
            P("student", "ctx", None),
            P("student", "ctx", None),
            P("student", "ctx", None),
            P("student", None, None),
            P("ctx", "student"),
            P("student", None),
            P(),
        ),
        out_specs=(P("student", "ctx", None), P("student", "ctx", None)),
        check_vma=False,
    )
```

```python
import math

import jax
import jax.numpy as jnp
from jax import lax
from jax.experimental import pallas as pl
from jax.experimental.pallas import tpu as pltpu
from jax.sharding import PartitionSpec as P

F32 = jnp.float32
BF16 = jnp.bfloat16
N = 32
HD = 128
SCALE = HD**-0.5 * math.log2(math.e)
ERR = 1.0 / math.sqrt(8192.0)
NEG = -1e30
GROUPS = 8
M = 512
CW = 1024
MESH = pl.DeviceIdType.MESH


def kernel(
    q, k, v, li, w, te, tm, order,
    sh_recv, wg_out_v,
    li_v, w_v, te_v, tm_v, kv, q_recv, qp, kpos, vp, att, d_home, d_recv, dpos,
    tp, tx, tt, th, th_recv, mg, aw, sh_send, wg_send, wa_recv, wb_send,
    sa, sb, m_ref, acc,
    loc, loc_tm, s1_s, s1_r, g_s, g_r, q_s, q_r, t_s, t_r, d_s, d_r,
    ag_s, ag_r, sh_s, sh_r, wa_s, wa_r, wb_s, wb_r,
):
    stu = lax.axis_index("student")
    me = lax.axis_index("ctx")
    core = lax.rem(stu, 2)
    xlo = stu // 2
    xh = me // 16
    mid, low = lax.rem(me // 4, 4), lax.rem(me, 4)
    a = jnp.where(core == 0, low, mid)
    b = jnp.where(core == 0, mid, low)
    t = xh * 4 + b
    mine = xh * 16 + b * 4 + a

    def ctx_of(x_, a_, b_):
        return x_ * 16 + jnp.where(core == 0, b_ * 4 + a_, a_ * 4 + b_)

    def remote(src, dst, ss, rs, where):
        return pltpu.make_async_remote_copy(
            src_ref=src, dst_ref=dst, send_sem=ss, recv_sem=rs, device_id=where, device_id_type=MESH
        )

    def cols(i, width):
        return pl.ds(pl.multiple_of(i * width, width), width)

    def peer(kk, sign):
        dx, db, da = kk // 16, lax.rem(kk // 4, 4), lax.rem(kk, 4)
        x_ = lax.rem(xh + dx, 2)
        a_ = lax.rem(a + sign * da + 4, 4)
        b_ = lax.rem(b + sign * db + 4, 4)
        return x_, a_, b_

    tm_loads = [
        pltpu.make_async_copy(tm.at[:, pl.ds(512 * i, 512)], tm_v.at[i % 2], loc_tm.at[i % 2])
        for i in range(4)
    ]
    c_te = pltpu.make_async_copy(te, te_v, loc.at[0])
    c_li = pltpu.make_async_copy(li, li_v, loc.at[1])
    c_w = pltpu.make_async_copy(w.at[:, cols(a, 512)], w_v, loc.at[2])
    c_k = pltpu.make_async_copy(k.at[:, :, cols(a, HD)], kv.at[mine, 0], loc.at[3])
    c_v = pltpu.make_async_copy(v.at[:, :, cols(a, HD)], kv.at[mine, 1], loc.at[4])
    c_q = pltpu.make_async_copy(q.at[:, cols(t, 16), cols(a, 512)], q_recv.at[mine], loc.at[5])
    for c in (c_k, c_v, c_q, c_te, tm_loads[0], tm_loads[1], c_li, c_w):
        c.start()

    barrier = pltpu.get_barrier_semaphore()

    def greet(i, _):
        pl.semaphore_signal(barrier, inc=1, device_id={"ctx": lax.rem(me + i, N)}, device_id_type=MESH)
        return 0

    lax.fori_loop(1, N, greet, 0)
    pair_core = {"student": xlo * 2 + 1 - core}
    pair_xlo = {"student": (1 - xlo) * 2 + core}
    pl.semaphore_signal(barrier, inc=1, device_id=pair_core, device_id_type=MESH)
    pl.semaphore_signal(barrier, inc=1, device_id=pair_xlo, device_id_type=MESH)
    pl.semaphore_wait(barrier, N + 1)

    firsts = []
    for da in range(1, 4):
        to = lax.rem(a + da, 4)
        for i, src in enumerate((k, v)):
            firsts.append(
                remote(
                    src.at[:, :, cols(to, HD)], kv.at[mine, i], s1_s.at[da, i], s1_r.at[da, i],
                    {"ctx": ctx_of(xh, to, b)},
                )
            )
    for c in firsts:
        c.start()

    def q_copy(kk, sign=1):
        x_, a_, b_ = peer(kk, sign)
        return remote(
            q.at[:, cols(x_ * 4 + b_, 16), cols(a_, 512)], q_recv.at[mine], q_s.at[kk], q_r.at[kk],
            {"ctx": ctx_of(x_, a_, b_)},
        )

    def q_start(kk, _):
        q_copy(kk).start()
        return 0

    lax.fori_loop(1, N, q_start, 0)
    c_k.wait()
    c_v.wait()
    for da in range(1, 4):
        frm = lax.rem(a - da + 4, 4)
        for i in range(2):
            at = kv.at[xh * 16 + b * 4 + frm, i]
            remote(at, at, s1_s.at[da, i], s1_r.at[da, i], {"ctx": ctx_of(xh, frm, b)}).wait_recv()
    right, left, across = lax.rem(b + 1, 4), lax.rem(b + 3, 4), lax.rem(b + 2, 4)

    def kv_rows(x_, b_, first, count):
        return kv.at[pl.ds(x_ * 16 + b_ * 4 + first, count)]

    def kv_copy(n, x_from, b_from, first, count, x_to, b_to):
        at = kv_rows(x_from, b_from, first, count)
        return remote(at, at, g_s.at[n], g_r.at[n], {"ctx": ctx_of(x_to, a, b_to)})

    xo = 1 - xh
    sent = []

    def send(*args):
        c = kv_copy(*args)
        c.start()
        sent.append(c)

    def arrive(*args):
        kv_copy(*args).wait_recv()

    send(0, xh, b, 0, 4, xo, b)
    send(1, xh, b, 0, 4, xh, right)
    send(2, xh, b, 0, 4, xh, left)

    vp[:, HD:] = jnp.ones((8192, HD), BF16)
    c_te.wait()
    for i in range(4):
        tm_loads[i].wait()
        tp[:, 512 * i : 512 * i + 512] = jnp.dot(te_v[...], tm_v[i % 2], preferred_element_type=F32)
        if i < 2:
            tm_loads[i + 2].start()
    half = pl.ds(pl.multiple_of(core * 128, 128), 128)
    half2 = pl.ds(pl.multiple_of((1 - core) * 128, 128), 128)
    t1 = remote(tp.at[half2], tx, t_s.at[0], t_r.at[0], pair_core)
    t1.start()
    t1.wait()
    th[...] = (tp[half, :] + tx[...]).astype(BF16)
    t2 = remote(th, th_recv, t_s.at[1], t_r.at[1], pair_xlo)
    t2.start()

    arrive(0, xo, b, 0, 4, xo, b)
    send(3, xo, b, 0, 4, xh, right)
    send(4, xo, b, 0, 4, xh, left)
    arrive(1, xh, left, 0, 4, xh, left)
    send(5, xh, left, 0, 2, xh, right)
    arrive(2, xh, right, 0, 4, xh, right)
    send(6, xh, right, 2, 2, xh, left)
    t2.wait()
    tp[half, :] = tp[half, :] + tx[...] + th_recv[...].astype(F32)
    t3 = remote(tp.at[half], tt, t_s.at[2], t_r.at[2], pair_core)
    t3.start()
    c_li.wait()
    d_home[core] = (li_v[core].astype(F32) - tp[half, :]).astype(BF16)
    t3.wait()
    d_home[1 - core] = (li_v[1 - core].astype(F32) - tt[...]).astype(BF16)

    arrive(3, xo, left, 0, 4, xh, left)
    send(7, xo, left, 0, 2, xh, right)
    arrive(4, xo, right, 0, 4, xh, right)
    send(8, xo, right, 2, 2, xh, left)
    c_q.wait()

    def q_wait(kk, _):
        x_, a_, b_ = peer(kk, -1)
        at = q_recv.at[x_ * 16 + b_ * 4 + a_]
        remote(at, at, q_s.at[kk], q_r.at[kk], {"ctx": ctx_of(x_, a_, b_)}).wait_recv()
        return 0

    lax.fori_loop(1, N, q_wait, 0)
    arrive(5, xh, across, 0, 2, xh, left)
    arrive(6, xh, across, 2, 2, xh, right)
    arrive(7, xo, across, 0, 2, xh, left)
    arrive(8, xo, across, 2, 2, xh, right)

    def d_copy(kk):
        x_, a_, b_ = peer(kk, 1)
        return remote(
            d_home.at[:, cols(x_ * 4 + b_, 16), cols(a_, 512)], d_recv.at[mine], d_s.at[kk], d_r.at[kk],
            {"ctx": ctx_of(x_, a_, b_)},
        )

    def d_start(kk, _):
        d_copy(kk).start()
        return 0

    lax.fori_loop(1, N, d_start, 0)
    d_recv[mine] = d_home[:, cols(t, 16), cols(a, 512)]

    def arrange(p, _):
        at = order[64 + p]
        part = order[128 + p]
        to = pl.ds(pl.multiple_of(p * 128, 128), 128)
        kpos[to, :] = kv[at, 0, part]
        vp[to, :HD] = kv[at, 1, part]
        slab = q_recv[at, part]
        for h in range(4):
            qp[p // 8, h, pl.ds(pl.multiple_of(lax.rem(p, 8) * 16, 16), 16), :] = slab[:, h * HD : h * HD + HD]
        return 0

    lax.fori_loop(0, 64, arrange, 0)

    def score(g, j, dst):
        dst[...] = lax.dot_general(
            qp[g].reshape(M, HD), kpos[cols(j, CW), :], (((1,), (1,)), ((), ())), preferred_element_type=F32
        )

    def absorb(src, j, diagonal=False):
        s = src[...]
        if diagonal:
            row = lax.rem(lax.broadcasted_iota(jnp.int32, (M, CW), 0), 128)
            col = lax.broadcasted_iota(jnp.int32, (M, CW), 1)
            s = jnp.where(col <= (row // 16) * 128 + t * 16 + lax.rem(row, 16), s, NEG)
        old = m_ref[...]
        new = jnp.maximum(old, jnp.max(s, axis=1, keepdims=True))
        m_ref[...] = new
        factor = jnp.exp2((old - new) * SCALE)
        p = jnp.exp2(s * SCALE - jnp.tile(new * SCALE, (1, CW // 128))).astype(BF16)
        acc[...] = acc[...] * jnp.tile(factor, (1, 2)) + jnp.dot(
            p, vp[cols(j, CW), :], preferred_element_type=F32
        )

    def begin():
        m_ref[...] = jnp.full((M, 128), NEG, F32)
        acc[...] = jnp.zeros((M, 256), F32)

    def att_copy(g, da):
        at = att.at[cols(g, 128), cols(a, 512)]
        return remote(at, at, ag_s.at[g, da], ag_r.at[g, da], {"ctx": ctx_of(xh, lax.rem(a + da, 4), b)})

    def finish(g):
        for h in range(4):
            rows = slice(h * 128, h * 128 + 128)
            att[cols(g, 128), pl.ds(pl.multiple_of(a * 512 + h * 128, 128), 128)] = (
                acc[rows, :HD] / acc[rows, HD:]
            ).astype(BF16)
        for da in range(1, 4):
            att_copy(g, da).start()

    def two_groups(u, _):
        g = 2 * u
        begin()
        score(g, 0, sa)

        def even(i, _):
            score(g, 2 * i + 1, sb)
            absorb(sa, 2 * i)
            score(g, 2 * i + 2, sa)
            absorb(sb, 2 * i + 1)
            return 0

        lax.fori_loop(0, u, even, 0)
        score(g + 1, 0, sb)
        absorb(sa, g, True)
        finish(g)
        begin()

        def odd(i, _):
            score(g + 1, 2 * i + 1, sa)
            absorb(sb, 2 * i)
            score(g + 1, 2 * i + 2, sb)
            absorb(sa, 2 * i + 1)
            return 0

        lax.fori_loop(0, u, odd, 0)
        score(g + 1, g + 1, sa)
        absorb(sb, g)
        absorb(sa, g + 1, True)
        finish(g + 1)
        return 0

    lax.fori_loop(0, GROUPS // 2, two_groups, 0)

    def d_wait(kk, _):
        x_, a_, b_ = peer(kk, -1)
        at = d_recv.at[x_ * 16 + b_ * 4 + a_]
        remote(at, at, d_s.at[kk], d_r.at[kk], {"ctx": ctx_of(x_, a_, b_)}).wait_recv()
        return 0

    lax.fori_loop(1, N, d_wait, 0)

    def arrange_d(p, _):
        dpos[cols(p, 16), :] = d_recv[order[64 + p], order[128 + p]]
        return 0

    lax.fori_loop(0, 64, arrange_d, 0)
    c_w.wait()

    def project(i, _):
        for g2 in range(2):
            g = 2 * i + g2
            for da in range(1, 4):
                frm = lax.rem(a - da + 4, 4)
                at = att.at[cols(g, 128), cols(frm, 512)]
                remote(at, at, ag_s.at[g, da], ag_r.at[g, da], {"ctx": ctx_of(xh, frm, b)}).wait_recv()
        rows = cols(i, 256)
        x = jnp.dot(att[rows, :], w_v[...], preferred_element_type=F32)
        aw[pl.ds(16 * i, 16)] = x.astype(BF16).reshape(16, 16, 512)
        mg[rows, :] = ((x + dpos[rows, :].astype(F32)) * ERR).astype(BF16)
        return 0

    lax.fori_loop(0, 4, project, 0)

    def arrange_sh(blk, _):
        sh_send[blk // 2, lax.rem(blk, 2)] = aw[order[blk]]
        return 0

    lax.fori_loop(0, 64, arrange_sh, 0)

    def sh_copy(kk):
        x_, a_, b_ = peer(kk, 1)
        to = ctx_of(x_, a_, b_)
        return remote(
            sh_send.at[to], sh_recv.at[:, cols(t, 16), cols(a, 512)], sh_s.at[kk], sh_r.at[kk], {"ctx": to}
        )

    def sh_start(kk, _):
        sh_copy(kk).start()
        return 0

    lax.fori_loop(1, N, sh_start, 0)
    sh_recv[:, cols(t, 16), cols(a, 512)] = sh_send[me]

    def wgrad(i, _):
        part = lax.dot_general(
            att[:, cols(i, 256)], mg[...], (((0,), (0,)), ((), ())), preferred_element_type=F32
        ).astype(BF16)
        for r in range(4):
            x_, mid_, low_ = i // 4, lax.rem(i, 4), r
            a_ = jnp.where(core == 0, low_, mid_)
            b_ = jnp.where(core == 0, mid_, low_)
            wg_send[x_, b_, a_] = part[r * 64 : r * 64 + 64]
        return 0

    lax.fori_loop(0, 8, wgrad, 0)

    def wa_copy(x_, db):
        to = lax.rem(b + db, 4)
        return remote(
            wg_send.at[x_, to], wa_recv.at[x_, db - 1], wa_s.at[x_, db], wa_r.at[x_, db],
            {"ctx": ctx_of(xh, a, to)},
        )

    for x_ in (xo, xh):
        for db in range(1, 4):
            wa_copy(x_, db).start()

    def wb_copy(da, far):
        to = lax.rem(a + da, 4)
        x_ = xo if far else xh
        return remote(
            wb_send.at[x_, to], wg_out_v.at[xh, :, cols(a, 512)], wb_s.at[far, da], wb_r.at[far, da],
            {"ctx": ctx_of(x_, to, b)},
        )

    for far in (1, 0):
        x_ = xo if far else xh
        for db in range(1, 4):
            frm = lax.rem(b - db + 4, 4)
            remote(
                wg_send.at[x_, frm], wa_recv.at[x_, db - 1], wa_s.at[x_, db], wa_r.at[x_, db],
                {"ctx": ctx_of(xh, a, frm)},
            ).wait_recv()
        for da in range(4):
            to = lax.rem(a + da, 4)
            total = wg_send[x_, b, to].astype(F32)
            for db in range(1, 4):
                total = total + wa_recv[x_, db - 1, to].astype(F32)
            if far == 0 and da == 0:
                wg_out_v[xh, :, cols(a, 512)] = total.astype(BF16)
            else:
                wb_send[x_, to] = total.astype(BF16)
                wb_copy(da, far).start()

    def sh_wait(kk, _):
        x_, a_, b_ = peer(kk, -1)
        at = sh_recv.at[:, cols(x_ * 4 + b_, 16), cols(a_, 512)]
        remote(sh_send.at[0], at, sh_s.at[kk], sh_r.at[kk], {"ctx": ctx_of(x_, a_, b_)}).wait_recv()
        return 0

    lax.fori_loop(1, N, sh_wait, 0)
    for far in (1, 0):
        x_ = xo if far else xh
        for da in range(4):
            if far == 0 and da == 0:
                continue
            frm = lax.rem(a - da + 4, 4)
            remote(
                wb_send.at[x_, frm], wg_out_v.at[x_, :, cols(frm, 512)], wb_s.at[far, da], wb_r.at[far, da],
                {"ctx": ctx_of(x_, frm, b)},
            ).wait_recv()

    for c in firsts + sent:
        c.wait_send()

    def drain(kk, _):
        q_copy(kk).wait_send()
        d_copy(kk).wait_send()
        sh_copy(kk).wait_send()
        return 0

    lax.fori_loop(1, N, drain, 0)

    def drain_att(g, _):
        for da in range(1, 4):
            att_copy(g, da).wait_send()
        return 0

    lax.fori_loop(0, GROUPS, drain_att, 0)
    for x_ in (xo, xh):
        for db in range(1, 4):
            wa_copy(x_, db).wait_send()
    for far in (1, 0):
        for da in range(4):
            if far or da:
                wb_copy(da, far).wait_send()


def local(query_states, key_states, value_states, layer_inputs, out_weight, teacher, teacher_map, offsets):
    pos = offsets // 128
    ids = jnp.arange(64, dtype=jnp.int32)
    inv = jnp.sum(jnp.where(pos[None, :] == ids[:, None], ids[None, :], 0), axis=1)
    home = inv // 2
    swapped = (home // 16) * 16 + (home % 4) * 4 + (home // 4) % 4
    slot = jnp.where(lax.axis_index("student") % 2 == 0, home, swapped)
    order = jnp.concatenate([pos, slot, inv % 2])
    hbm = pl.BlockSpec(memory_space=pl.ANY)
    vmem = pl.BlockSpec(memory_space=pltpu.VMEM)
    dma = pltpu.SemaphoreType.DMA
    sh, wg = pl.pallas_call(
        kernel,
        name="layer",
        out_shape=(
            jax.ShapeDtypeStruct((2, 128, 2048), BF16),
            jax.ShapeDtypeStruct((2, 64, 2048), BF16),
        ),
        in_specs=[hbm] * 7 + [pl.BlockSpec(memory_space=pltpu.SMEM)],
        out_specs=(vmem, vmem),
        scratch_shapes=[
            pltpu.VMEM((2, 128, 2048), BF16),
            pltpu.VMEM((2048, 512), BF16),
            pltpu.VMEM((256, 2048), BF16),
            pltpu.VMEM((2, 2048, 512), BF16),
            pltpu.VMEM((32, 2, 2, 128, 128), BF16),
            pltpu.VMEM((32, 2, 16, 512), BF16),
            pltpu.VMEM((GROUPS, 4, 128, 128), BF16),
            pltpu.VMEM((8192, 128), BF16),
            pltpu.VMEM((8192, 256), BF16),
            pltpu.VMEM((1024, 2048), BF16),
            pltpu.VMEM((2, 128, 2048), BF16),
            pltpu.VMEM((32, 2, 16, 512), BF16),
            pltpu.VMEM((1024, 512), BF16),
            pltpu.VMEM((256, 2048), F32),
            pltpu.VMEM((128, 2048), F32),
            pltpu.VMEM((128, 2048), F32),
            pltpu.VMEM((128, 2048), BF16),
            pltpu.VMEM((128, 2048), BF16),
            pltpu.VMEM((1024, 512), BF16),
            pltpu.VMEM((64, 16, 512), BF16),
            pltpu.VMEM((32, 2, 16, 512), BF16),
            pltpu.VMEM((2, 4, 4, 64, 512), BF16),
            pltpu.VMEM((2, 3, 4, 64, 512), BF16),
            pltpu.VMEM((2, 4, 64, 512), BF16),
            pltpu.VMEM((M, CW), F32),
            pltpu.VMEM((M, CW), F32),
            pltpu.VMEM((M, 128), F32),
            pltpu.VMEM((M, 256), F32),
            dma((6,)), dma((2,)),
            dma((4, 2)), dma((4, 2)),
            dma((9,)), dma((9,)),
            dma((N,)), dma((N,)), dma((3,)), dma((3,)), dma((N,)), dma((N,)),
            dma((GROUPS, 4)), dma((GROUPS, 4)),
            dma((N,)), dma((N,)), dma((2, 4)), dma((2, 4)), dma((2, 4)), dma((2, 4)),
        ],
        compiler_params=pltpu.CompilerParams(
            collective_id=0, has_side_effects=True, vmem_limit_bytes=60 * 1024 * 1024
        ),
    )(
        query_states[0].reshape(2, 128, 2048), key_states[0].reshape(2, 128, 512), value_states[0].reshape(2, 128, 512),
        layer_inputs[0].reshape(2, 128, 2048), out_weight[0], teacher, teacher_map, order,
    )
    hidden = (layer_inputs[0].astype(F32) + sh.reshape(256, 2048).astype(F32)).astype(BF16)
    return hidden[None], (wg[0].astype(F32) + wg[1].astype(F32))[None]


def solution(mesh):
    return jax.shard_map(
        local,
        mesh=mesh,
        in_specs=(
            P("student", "ctx", None),
            P("student", "ctx", None),
            P("student", "ctx", None),
            P("student", "ctx", None),
            P("student", None, None),
            P("ctx", "student"),
            P("student", None),
            P(),
        ),
        out_specs=(P("student", "ctx", None), P("student", "ctx", None)),
        check_vma=False,
    )
```

```python
import math

import jax
import jax.numpy as jnp
from jax import lax
from jax.experimental import pallas as pl
from jax.experimental.pallas import tpu as pltpu
from jax.sharding import PartitionSpec as P

F32 = jnp.float32
BF16 = jnp.bfloat16
N = 32
HD = 128
SCALE = HD**-0.5 * math.log2(math.e)
ERR = 1.0 / math.sqrt(8192.0)
NEG = -1e30
GROUPS = 8
M = 512
CW = 1024
MESH = pl.DeviceIdType.MESH


def kernel(
    q, k, v, li, w, te, tm, order,
    sh_recv, wg_out_v,
    li_v, w_v, te_v, tm_v, kv, q_recv, qp, kpos, vp, att, d_home, d_recv, dpos,
    tp, tx, tt, th, th_recv, mg, aw, sh_send, wg_send, wa_recv, wb_send,
    sa, sb, m_ref, acc,
    loc, loc_tm, s1_s, s1_r, g_s, g_r, q_s, q_r, t_s, t_r, d_s, d_r,
    ag_s, ag_r, sh_s, sh_r, wa_s, wa_r, wb_s, wb_r,
):
    stu = lax.axis_index("student")
    me = lax.axis_index("ctx")
    core = lax.rem(stu, 2)
    xlo = stu // 2
    xh = me // 16
    mid, low = lax.rem(me // 4, 4), lax.rem(me, 4)
    a = jnp.where(core == 0, low, mid)
    b = jnp.where(core == 0, mid, low)
    t = xh * 4 + b
    mine = xh * 16 + b * 4 + a

    def ctx_of(x_, a_, b_):
        return x_ * 16 + jnp.where(core == 0, b_ * 4 + a_, a_ * 4 + b_)

    def remote(src, dst, ss, rs, where):
        return pltpu.make_async_remote_copy(
            src_ref=src, dst_ref=dst, send_sem=ss, recv_sem=rs, device_id=where, device_id_type=MESH
        )

    def cols(i, width):
        return pl.ds(pl.multiple_of(i * width, width), width)

    def peer(kk, sign):
        dx, db, da = kk // 16, lax.rem(kk // 4, 4), lax.rem(kk, 4)
        x_ = lax.rem(xh + dx, 2)
        a_ = lax.rem(a + sign * da + 4, 4)
        b_ = lax.rem(b + sign * db + 4, 4)
        return x_, a_, b_

    tm_loads = [
        pltpu.make_async_copy(tm.at[:, pl.ds(512 * i, 512)], tm_v.at[i % 2], loc_tm.at[i % 2])
        for i in range(4)
    ]
    c_te = pltpu.make_async_copy(te, te_v, loc.at[0])
    c_li = pltpu.make_async_copy(li, li_v, loc.at[1])
    c_w = pltpu.make_async_copy(w.at[:, cols(a, 512)], w_v, loc.at[2])
    c_k = pltpu.make_async_copy(k.at[:, :, cols(a, HD)], kv.at[mine, 0], loc.at[3])
    c_v = pltpu.make_async_copy(v.at[:, :, cols(a, HD)], kv.at[mine, 1], loc.at[4])
    c_q = pltpu.make_async_copy(q.at[:, cols(t, 16), cols(a, 512)], q_recv.at[mine], loc.at[5])
    for c in (c_k, c_v, c_q, c_te, tm_loads[0], tm_loads[1], c_li, c_w):
        c.start()

    barrier = pltpu.get_barrier_semaphore()

    def greet(i, _):
        pl.semaphore_signal(barrier, inc=1, device_id={"ctx": lax.rem(me + i, N)}, device_id_type=MESH)
        return 0

    lax.fori_loop(1, N, greet, 0)
    pair_core = {"student": xlo * 2 + 1 - core}
    pair_xlo = {"student": (1 - xlo) * 2 + core}
    pl.semaphore_signal(barrier, inc=1, device_id=pair_core, device_id_type=MESH)
    pl.semaphore_signal(barrier, inc=1, device_id=pair_xlo, device_id_type=MESH)
    pl.semaphore_wait(barrier, N + 1)

    xo = 1 - xh
    right, left, across = lax.rem(b + 1, 4), lax.rem(b + 3, 4), lax.rem(b + 2, 4)
    sent = []

    def first_copy(far, da, i):
        to = lax.rem(a + da, 4)
        return remote(
            (k, v)[i].at[:, :, cols(to, HD)], kv.at[mine, i], s1_s.at[far, da, i], s1_r.at[far, da, i],
            {"ctx": ctx_of(xo if far else xh, to, b)},
        )

    for far, da in ((0, 1), (1, 0), (0, 2), (1, 1), (0, 3), (1, 2), (1, 3)):
        for i in range(2):
            c = first_copy(far, da, i)
            c.start()
            sent.append(c)

    def piece(far, r, b_):
        return kv.at[(xo if far else xh) * 16 + b_ * 4 + lax.rem(a - r + 4, 4)]

    def hop(far, r, way, b_):
        at = piece(far, r, b_)
        return remote(
            at, at, g_s.at[far, r, way], g_r.at[far, r, way], {"ctx": ctx_of(xh, a, left if way % 2 else right)}
        )

    def pass_on(far, r):
        for i in range(2):
            if far or r:
                at = piece(far, r, b).at[i]
                remote(at, at, s1_s.at[far, r, i], s1_r.at[far, r, i], {"ctx": ctx_of(xh, a, right)}).wait_recv()
        for way in range(2):
            c = hop(far, r, way, b)
            c.start()
            sent.append(c)

    def relay(far, r):
        way = r % 2
        frm = right if way else left
        hop(far, r, way, frm).wait_recv()
        c = hop(far, r, 2 + way, frm)
        c.start()
        sent.append(c)

    def q_copy(kk, sign=1):
        x_, a_, b_ = peer(kk, sign)
        return remote(
            q.at[:, cols(x_ * 4 + b_, 16), cols(a_, 512)], q_recv.at[mine], q_s.at[kk], q_r.at[kk],
            {"ctx": ctx_of(x_, a_, b_)},
        )

    def q_start(kk, _):
        q_copy(kk).start()
        return 0

    c_k.wait()
    c_v.wait()
    pass_on(0, 0)
    lax.fori_loop(1, N, q_start, 0)
    vp[:, HD:] = jnp.ones((8192, HD), BF16)
    for r in range(1, 4):
        pass_on(0, r)
    c_te.wait()
    for i in range(4):
        tm_loads[i].wait()
        tp[:, 512 * i : 512 * i + 512] = jnp.dot(te_v[...], tm_v[i % 2], preferred_element_type=F32)
        if i < 2:
            tm_loads[i + 2].start()
        pass_on(1, i)
    half = pl.ds(pl.multiple_of(core * 128, 128), 128)
    half2 = pl.ds(pl.multiple_of((1 - core) * 128, 128), 128)
    t1 = remote(tp.at[half2], tx, t_s.at[0], t_r.at[0], pair_core)
    t1.start()
    for r in range(4):
        relay(0, r)
    t1.wait()
    tp[half, :] = tp[half, :] + tx[...]
    th[...] = tp[half, :].astype(BF16)
    t2 = remote(th, th_recv, t_s.at[1], t_r.at[1], pair_xlo)
    t2.start()
    for r in range(4):
        relay(1, r)
    t2.wait()
    tp[half, :] = tp[half, :] + th_recv[...].astype(F32)
    t3 = remote(tp.at[half], tt, t_s.at[2], t_r.at[2], pair_core)
    t3.start()
    c_li.wait()
    d_home[core] = (li_v[core].astype(F32) - tp[half, :]).astype(BF16)

    c_q.wait()

    def q_wait(kk, _):
        x_, a_, b_ = peer(kk, -1)
        at = q_recv.at[x_ * 16 + b_ * 4 + a_]
        remote(at, at, q_s.at[kk], q_r.at[kk], {"ctx": ctx_of(x_, a_, b_)}).wait_recv()
        return 0

    lax.fori_loop(1, N, q_wait, 0)
    for far in range(2):
        for r in range(4):
            way = 1 - r % 2
            hop(far, r, way, right if way else left).wait_recv()
            hop(far, r, 2 + r % 2, across).wait_recv()
    t3.wait()
    d_home[1 - core] = (li_v[1 - core].astype(F32) - tt[...]).astype(BF16)

    def d_copy(kk):
        x_, a_, b_ = peer(kk, 1)
        return remote(
            d_home.at[:, cols(x_ * 4 + b_, 16), cols(a_, 512)], d_recv.at[mine], d_s.at[kk], d_r.at[kk],
            {"ctx": ctx_of(x_, a_, b_)},
        )

    def d_start(kk, _):
        d_copy(kk).start()
        return 0

    lax.fori_loop(1, N, d_start, 0)
    d_recv[mine] = d_home[:, cols(t, 16), cols(a, 512)]

    def arrange(p, _):
        at = order[64 + p]
        part = order[128 + p]
        to = pl.ds(pl.multiple_of(p * 128, 128), 128)
        kpos[to, :] = kv[at, 0, part]
        vp[to, :HD] = kv[at, 1, part]
        slab = q_recv[at, part]
        for h in range(4):
            qp[p // 8, h, pl.ds(pl.multiple_of(lax.rem(p, 8) * 16, 16), 16), :] = slab[:, h * HD : h * HD + HD]
        return 0

    lax.fori_loop(0, 64, arrange, 0)

    def score(g, j, dst):
        dst[...] = lax.dot_general(
            qp[g].reshape(M, HD), kpos[cols(j, CW), :], (((1,), (1,)), ((), ())), preferred_element_type=F32
        )

    def absorb(src, j, diagonal=False):
        s = src[...]
        if diagonal:
            row = lax.rem(lax.broadcasted_iota(jnp.int32, (M, CW), 0), 128)
            col = lax.broadcasted_iota(jnp.int32, (M, CW), 1)
            s = jnp.where(col <= (row // 16) * 128 + t * 16 + lax.rem(row, 16), s, NEG)
        old = m_ref[...]
        new = jnp.maximum(old, jnp.max(s, axis=1, keepdims=True))
        m_ref[...] = new
        factor = jnp.exp2((old - new) * SCALE)
        p = jnp.exp2(s * SCALE - jnp.tile(new * SCALE, (1, CW // 128))).astype(BF16)
        acc[...] = acc[...] * jnp.tile(factor, (1, 2)) + jnp.dot(
            p, vp[cols(j, CW), :], preferred_element_type=F32
        )

    def begin():
        m_ref[...] = jnp.full((M, 128), NEG, F32)
        acc[...] = jnp.zeros((M, 256), F32)

    def att_copy(g, da):
        at = att.at[cols(g, 128), cols(a, 512)]
        return remote(at, at, ag_s.at[g, da], ag_r.at[g, da], {"ctx": ctx_of(xh, lax.rem(a + da, 4), b)})

    def finish(g):
        for h in range(4):
            rows = slice(h * 128, h * 128 + 128)
            att[cols(g, 128), pl.ds(pl.multiple_of(a * 512 + h * 128, 128), 128)] = (
                acc[rows, :HD] / acc[rows, HD:]
            ).astype(BF16)
        for da in range(1, 4):
            att_copy(g, da).start()

    def two_groups(u, _):
        g = 2 * u
        begin()
        score(g, 0, sa)

        def even(i, _):
            score(g, 2 * i + 1, sb)
            absorb(sa, 2 * i)
            score(g, 2 * i + 2, sa)
            absorb(sb, 2 * i + 1)
            return 0

        lax.fori_loop(0, u, even, 0)
        score(g + 1, 0, sb)
        absorb(sa, g, True)
        finish(g)
        begin()

        def odd(i, _):
            score(g + 1, 2 * i + 1, sa)
            absorb(sb, 2 * i)
            score(g + 1, 2 * i + 2, sb)
            absorb(sa, 2 * i + 1)
            return 0

        lax.fori_loop(0, u, odd, 0)
        score(g + 1, g + 1, sa)
        absorb(sb, g)
        absorb(sa, g + 1, True)
        finish(g + 1)
        return 0

    lax.fori_loop(0, GROUPS // 2, two_groups, 0)

    def d_wait(kk, _):
        x_, a_, b_ = peer(kk, -1)
        at = d_recv.at[x_ * 16 + b_ * 4 + a_]
        remote(at, at, d_s.at[kk], d_r.at[kk], {"ctx": ctx_of(x_, a_, b_)}).wait_recv()
        return 0

    lax.fori_loop(1, N, d_wait, 0)

    def arrange_d(p, _):
        dpos[cols(p, 16), :] = d_recv[order[64 + p], order[128 + p]]
        return 0

    lax.fori_loop(0, 64, arrange_d, 0)
    c_w.wait()

    def project(i, _):
        for g2 in range(2):
            g = 2 * i + g2
            for da in range(1, 4):
                frm = lax.rem(a - da + 4, 4)
                at = att.at[cols(g, 128), cols(frm, 512)]
                remote(at, at, ag_s.at[g, da], ag_r.at[g, da], {"ctx": ctx_of(xh, frm, b)}).wait_recv()
        rows = cols(i, 256)
        x = jnp.dot(att[rows, :], w_v[...], preferred_element_type=F32)
        aw[pl.ds(16 * i, 16)] = x.astype(BF16).reshape(16, 16, 512)
        mg[rows, :] = ((x + dpos[rows, :].astype(F32)) * ERR).astype(BF16)
        return 0

    lax.fori_loop(0, 4, project, 0)

    def arrange_sh(blk, _):
        sh_send[blk // 2, lax.rem(blk, 2)] = aw[order[blk]]
        return 0

    lax.fori_loop(0, 64, arrange_sh, 0)

    def sh_copy(kk):
        x_, a_, b_ = peer(kk, 1)
        to = ctx_of(x_, a_, b_)
        return remote(
            sh_send.at[to], sh_recv.at[:, cols(t, 16), cols(a, 512)], sh_s.at[kk], sh_r.at[kk], {"ctx": to}
        )

    def sh_start(kk, _):
        sh_copy(kk).start()
        return 0

    lax.fori_loop(1, N, sh_start, 0)
    sh_recv[:, cols(t, 16), cols(a, 512)] = sh_send[me]

    def wgrad(i, _):
        part = lax.dot_general(
            att[:, cols(i, 256)], mg[...], (((0,), (0,)), ((), ())), preferred_element_type=F32
        ).astype(BF16)
        for r in range(4):
            x_, mid_, low_ = i // 4, lax.rem(i, 4), r
            a_ = jnp.where(core == 0, low_, mid_)
            b_ = jnp.where(core == 0, mid_, low_)
            wg_send[x_, b_, a_] = part[r * 64 : r * 64 + 64]
        return 0

    lax.fori_loop(0, 8, wgrad, 0)

    def wa_copy(x_, db):
        to = lax.rem(b + db, 4)
        return remote(
            wg_send.at[x_, to], wa_recv.at[x_, db - 1], wa_s.at[x_, db], wa_r.at[x_, db],
            {"ctx": ctx_of(xh, a, to)},
        )

    for x_ in (xo, xh):
        for db in range(1, 4):
            wa_copy(x_, db).start()

    def wb_copy(da, far):
        to = lax.rem(a + da, 4)
        x_ = xo if far else xh
        return remote(
            wb_send.at[x_, to], wg_out_v.at[xh, :, cols(a, 512)], wb_s.at[far, da], wb_r.at[far, da],
            {"ctx": ctx_of(x_, to, b)},
        )

    for far in (1, 0):
        x_ = xo if far else xh
        for db in range(1, 4):
            frm = lax.rem(b - db + 4, 4)
            remote(
                wg_send.at[x_, frm], wa_recv.at[x_, db - 1], wa_s.at[x_, db], wa_r.at[x_, db],
                {"ctx": ctx_of(xh, a, frm)},
            ).wait_recv()
        for da in range(4):
            to = lax.rem(a + da, 4)
            total = wg_send[x_, b, to].astype(F32)
            for db in range(1, 4):
                total = total + wa_recv[x_, db - 1, to].astype(F32)
            if far == 0 and da == 0:
                wg_out_v[xh, :, cols(a, 512)] = total.astype(BF16)
            else:
                wb_send[x_, to] = total.astype(BF16)
                wb_copy(da, far).start()

    def sh_wait(kk, _):
        x_, a_, b_ = peer(kk, -1)
        at = sh_recv.at[:, cols(x_ * 4 + b_, 16), cols(a_, 512)]
        remote(sh_send.at[0], at, sh_s.at[kk], sh_r.at[kk], {"ctx": ctx_of(x_, a_, b_)}).wait_recv()
        return 0

    lax.fori_loop(1, N, sh_wait, 0)
    for far in (1, 0):
        x_ = xo if far else xh
        for da in range(4):
            if far == 0 and da == 0:
                continue
            frm = lax.rem(a - da + 4, 4)
            remote(
                wb_send.at[x_, frm], wg_out_v.at[x_, :, cols(frm, 512)], wb_s.at[far, da], wb_r.at[far, da],
                {"ctx": ctx_of(x_, frm, b)},
            ).wait_recv()

    for c in sent:
        c.wait_send()

    def drain(kk, _):
        q_copy(kk).wait_send()
        d_copy(kk).wait_send()
        sh_copy(kk).wait_send()
        return 0

    lax.fori_loop(1, N, drain, 0)

    def drain_att(g, _):
        for da in range(1, 4):
            att_copy(g, da).wait_send()
        return 0

    lax.fori_loop(0, GROUPS, drain_att, 0)
    for x_ in (xo, xh):
        for db in range(1, 4):
            wa_copy(x_, db).wait_send()
    for far in (1, 0):
        for da in range(4):
            if far or da:
                wb_copy(da, far).wait_send()


def local(query_states, key_states, value_states, layer_inputs, out_weight, teacher, teacher_map, offsets):
    pos = offsets // 128
    ids = jnp.arange(64, dtype=jnp.int32)
    inv = jnp.sum(jnp.where(pos[None, :] == ids[:, None], ids[None, :], 0), axis=1)
    home = inv // 2
    swapped = (home // 16) * 16 + (home % 4) * 4 + (home // 4) % 4
    slot = jnp.where(lax.axis_index("student") % 2 == 0, home, swapped)
    order = jnp.concatenate([pos, slot, inv % 2])
    hbm = pl.BlockSpec(memory_space=pl.ANY)
    vmem = pl.BlockSpec(memory_space=pltpu.VMEM)
    dma = pltpu.SemaphoreType.DMA
    sh, wg = pl.pallas_call(
        kernel,
        name="layer",
        out_shape=(
            jax.ShapeDtypeStruct((2, 128, 2048), BF16),
            jax.ShapeDtypeStruct((2, 64, 2048), BF16),
        ),
        in_specs=[hbm] * 7 + [pl.BlockSpec(memory_space=pltpu.SMEM)],
        out_specs=(vmem, vmem),
        scratch_shapes=[
            pltpu.VMEM((2, 128, 2048), BF16),
            pltpu.VMEM((2048, 512), BF16),
            pltpu.VMEM((256, 2048), BF16),
            pltpu.VMEM((2, 2048, 512), BF16),
            pltpu.VMEM((32, 2, 2, 128, 128), BF16),
            pltpu.VMEM((32, 2, 16, 512), BF16),
            pltpu.VMEM((GROUPS, 4, 128, 128), BF16),
            pltpu.VMEM((8192, 128), BF16),
            pltpu.VMEM((8192, 256), BF16),
            pltpu.VMEM((1024, 2048), BF16),
            pltpu.VMEM((2, 128, 2048), BF16),
            pltpu.VMEM((32, 2, 16, 512), BF16),
            pltpu.VMEM((1024, 512), BF16),
            pltpu.VMEM((256, 2048), F32),
            pltpu.VMEM((128, 2048), F32),
            pltpu.VMEM((128, 2048), F32),
            pltpu.VMEM((128, 2048), BF16),
            pltpu.VMEM((128, 2048), BF16),
            pltpu.VMEM((1024, 512), BF16),
            pltpu.VMEM((64, 16, 512), BF16),
            pltpu.VMEM((32, 2, 16, 512), BF16),
            pltpu.VMEM((2, 4, 4, 64, 512), BF16),
            pltpu.VMEM((2, 3, 4, 64, 512), BF16),
            pltpu.VMEM((2, 4, 64, 512), BF16),
            pltpu.VMEM((M, CW), F32),
            pltpu.VMEM((M, CW), F32),
            pltpu.VMEM((M, 128), F32),
            pltpu.VMEM((M, 256), F32),
            dma((6,)), dma((2,)),
            dma((2, 4, 2)), dma((2, 4, 2)),
            dma((2, 4, 4)), dma((2, 4, 4)),
            dma((N,)), dma((N,)), dma((3,)), dma((3,)), dma((N,)), dma((N,)),
            dma((GROUPS, 4)), dma((GROUPS, 4)),
            dma((N,)), dma((N,)), dma((2, 4)), dma((2, 4)), dma((2, 4)), dma((2, 4)),
        ],
        compiler_params=pltpu.CompilerParams(
            collective_id=0, has_side_effects=True, vmem_limit_bytes=60 * 1024 * 1024
        ),
    )(
        query_states[0].reshape(2, 128, 2048), key_states[0].reshape(2, 128, 512), value_states[0].reshape(2, 128, 512),
        layer_inputs[0].reshape(2, 128, 2048), out_weight[0], teacher, teacher_map, order,
    )
    hidden = (layer_inputs[0].astype(F32) + sh.reshape(256, 2048).astype(F32)).astype(BF16)
    return hidden[None], (wg[0].astype(F32) + wg[1].astype(F32))[None]


def solution(mesh):
    return jax.shard_map(
        local,
        mesh=mesh,
        in_specs=(
            P("student", "ctx", None),
            P("student", "ctx", None),
            P("student", "ctx", None),
            P("student", "ctx", None),
            P("student", None, None),
            P("ctx", "student"),
            P("student", None),
            P(),
        ),
        out_specs=(P("student", "ctx", None), P("student", "ctx", None)),
        check_vma=False,
    )
```

```python
import math

import jax
import jax.numpy as jnp
from jax import lax
from jax.experimental import pallas as pl
from jax.experimental.pallas import tpu as pltpu
from jax.sharding import PartitionSpec as P

F32 = jnp.float32
BF16 = jnp.bfloat16
N = 32
HD = 128
SCALE = HD**-0.5 * math.log2(math.e)
ERR = 1.0 / math.sqrt(8192.0)
NEG = -1e30
GROUPS = 8
M = 512
CW = 1024
MESH = pl.DeviceIdType.MESH


def kernel(
    q, k, v, li, w, te, tm, pos, where,
    sh_recv, wg_out_v,
    li_v, w_v, te_v, tm_v, kv, q_recv, qp, kpos, vp, att, d_home, d_recv, dpos,
    tp, tx, tt, th, th_recv, mg, aw, sh_send, wg_send, wa_recv, wb_send,
    sa, sb, ma, mb, m_ref, acc,
    loc, loc_tm, s1_s, s1_r, g_s, g_r, q_s, q_r, t_s, t_r, d_s, d_r,
    ag_s, ag_r, sh_s, sh_r, wa_s, wa_r, wb_s, wb_r,
):
    stu = lax.axis_index("student")
    me = lax.axis_index("ctx")
    core = lax.rem(stu, 2)
    xlo = stu // 2
    xh = me // 16
    mid, low = lax.rem(me // 4, 4), lax.rem(me, 4)
    a = jnp.where(core == 0, low, mid)
    b = jnp.where(core == 0, mid, low)
    t = xh * 4 + b
    mine = xh * 16 + b * 4 + a

    def ctx_of(x_, a_, b_):
        return x_ * 16 + jnp.where(core == 0, b_ * 4 + a_, a_ * 4 + b_)

    def remote(src, dst, ss, rs, target):
        return pltpu.make_async_remote_copy(
            src_ref=src, dst_ref=dst, send_sem=ss, recv_sem=rs, device_id=target, device_id_type=MESH
        )

    def cols(i, width):
        return pl.ds(pl.multiple_of(i * width, width), width)

    def peer(kk, sign):
        dx, db, da = kk // 16, lax.rem(kk // 4, 4), lax.rem(kk, 4)
        x_ = lax.rem(xh + dx, 2)
        a_ = lax.rem(a + sign * da + 4, 4)
        b_ = lax.rem(b + sign * db + 4, 4)
        return x_, a_, b_

    tm_loads = [
        pltpu.make_async_copy(tm.at[:, pl.ds(512 * i, 512)], tm_v.at[i % 2], loc_tm.at[i % 2])
        for i in range(4)
    ]
    c_te = pltpu.make_async_copy(te, te_v, loc.at[0])
    c_li = pltpu.make_async_copy(li, li_v, loc.at[1])
    c_w = pltpu.make_async_copy(w.at[:, cols(a, 512)], w_v, loc.at[2])
    c_k = pltpu.make_async_copy(k.at[:, :, cols(a, HD)], kv.at[pl.ds(2 * mine, 2), 0], loc.at[3])
    c_v = pltpu.make_async_copy(v.at[:, :, cols(a, HD)], kv.at[pl.ds(2 * mine, 2), 1], loc.at[4])
    c_q = pltpu.make_async_copy(q.at[:, cols(t, 16), cols(a, 512)], q_recv.at[pl.ds(2 * mine, 2)], loc.at[5])
    for c in (c_k, c_v, c_q, c_te, tm_loads[0], tm_loads[1], c_li, c_w):
        c.start()

    barrier = pltpu.get_barrier_semaphore()

    def greet(i, _):
        pl.semaphore_signal(barrier, inc=1, device_id={"ctx": lax.rem(me + i, N)}, device_id_type=MESH)
        return 0

    lax.fori_loop(1, N, greet, 0)
    pair_core = {"student": xlo * 2 + 1 - core}
    pair_xlo = {"student": (1 - xlo) * 2 + core}
    pl.semaphore_signal(barrier, inc=1, device_id=pair_core, device_id_type=MESH)
    pl.semaphore_signal(barrier, inc=1, device_id=pair_xlo, device_id_type=MESH)
    pl.semaphore_wait(barrier, N + 1)

    xo = 1 - xh
    right, left, across = lax.rem(b + 1, 4), lax.rem(b + 3, 4), lax.rem(b + 2, 4)
    sent = []

    def first_copy(far, da, i):
        to = lax.rem(a + da, 4)
        return remote(
            (k, v)[i].at[:, :, cols(to, HD)], kv.at[pl.ds(2 * mine, 2), i], s1_s.at[far, da, i], s1_r.at[far, da, i],
            {"ctx": ctx_of(xo if far else xh, to, b)},
        )

    for far, da in ((0, 1), (1, 0), (0, 2), (1, 1), (0, 3), (1, 2), (1, 3)):
        for i in range(2):
            c = first_copy(far, da, i)
            c.start()
            sent.append(c)

    def piece(far, r, b_):
        return kv.at[pl.ds(2 * ((xo if far else xh) * 16 + b_ * 4 + lax.rem(a - r + 4, 4)), 2)]

    def hop(far, r, way, b_):
        at = piece(far, r, b_)
        return remote(
            at, at, g_s.at[far, r, way], g_r.at[far, r, way], {"ctx": ctx_of(xh, a, left if way % 2 else right)}
        )

    def pass_on(far, r):
        for i in range(2):
            if far or r:
                at = piece(far, r, b).at[:, i]
                remote(at, at, s1_s.at[far, r, i], s1_r.at[far, r, i], {"ctx": ctx_of(xh, a, right)}).wait_recv()
        for way in range(2):
            c = hop(far, r, way, b)
            c.start()
            sent.append(c)

    def relay(far, r):
        way = r % 2
        frm = right if way else left
        hop(far, r, way, frm).wait_recv()
        c = hop(far, r, 2 + way, frm)
        c.start()
        sent.append(c)

    def q_copy(kk, sign=1):
        x_, a_, b_ = peer(kk, sign)
        return remote(
            q.at[:, cols(x_ * 4 + b_, 16), cols(a_, 512)], q_recv.at[pl.ds(2 * mine, 2)], q_s.at[kk], q_r.at[kk],
            {"ctx": ctx_of(x_, a_, b_)},
        )

    def q_start(kk, _):
        q_copy(kk).start()
        return 0

    c_k.wait()
    c_v.wait()
    pass_on(0, 0)
    lax.fori_loop(1, N, q_start, 0)
    vp[:, HD:] = jnp.ones((8192, HD), BF16)
    for r in range(1, 4):
        pass_on(0, r)
    c_te.wait()
    for i in range(4):
        tm_loads[i].wait()
        tp[:, 512 * i : 512 * i + 512] = jnp.dot(te_v[...], tm_v[i % 2], preferred_element_type=F32)
        if i < 2:
            tm_loads[i + 2].start()
        pass_on(1, i)
    half = pl.ds(pl.multiple_of(core * 128, 128), 128)
    half2 = pl.ds(pl.multiple_of((1 - core) * 128, 128), 128)
    t1 = remote(tp.at[half2], tx, t_s.at[0], t_r.at[0], pair_core)
    t1.start()
    for r in range(4):
        relay(0, r)
    t1.wait()
    tp[half, :] = tp[half, :] + tx[...]
    th[...] = tp[half, :].astype(BF16)
    t2 = remote(th, th_recv, t_s.at[1], t_r.at[1], pair_xlo)
    t2.start()
    for r in range(4):
        relay(1, r)
    t2.wait()
    tp[half, :] = tp[half, :] + th_recv[...].astype(F32)
    t3 = remote(tp.at[half], tt, t_s.at[2], t_r.at[2], pair_core)
    t3.start()
    c_li.wait()
    d_home[core] = (li_v[core].astype(F32) - tp[half, :]).astype(BF16)

    c_q.wait()

    def q_wait(kk, _):
        x_, a_, b_ = peer(kk, -1)
        at = q_recv.at[pl.ds(2 * (x_ * 16 + b_ * 4 + a_), 2)]
        remote(at, at, q_s.at[kk], q_r.at[kk], {"ctx": ctx_of(x_, a_, b_)}).wait_recv()
        return 0

    lax.fori_loop(1, N, q_wait, 0)
    for far in range(2):
        for r in range(4):
            way = 1 - r % 2
            hop(far, r, way, right if way else left).wait_recv()
            hop(far, r, 2 + r % 2, across).wait_recv()
    t3.wait()
    d_home[1 - core] = (li_v[1 - core].astype(F32) - tt[...]).astype(BF16)

    def d_copy(kk):
        x_, a_, b_ = peer(kk, 1)
        return remote(
            d_home.at[:, cols(x_ * 4 + b_, 16), cols(a_, 512)], d_recv.at[pl.ds(2 * mine, 2)], d_s.at[kk], d_r.at[kk],
            {"ctx": ctx_of(x_, a_, b_)},
        )

    def d_start(kk, _):
        d_copy(kk).start()
        return 0

    lax.fori_loop(1, N, d_start, 0)
    d_recv[pl.ds(2 * mine, 2)] = d_home[:, cols(t, 16), cols(a, 512)]

    def arrange(p, _):
        at = where[p]
        to = pl.ds(pl.multiple_of(p * 128, 128), 128)
        kpos[to, :] = kv[at, 0]
        vp[to, :HD] = kv[at, 1]
        slab = q_recv[at]
        for h in range(4):
            qp[p // 8, h, pl.ds(pl.multiple_of(lax.rem(p, 8) * 16, 16), 16), :] = slab[:, h * HD : h * HD + HD]
        return 0

    lax.fori_loop(0, 64, arrange, 0)

    def score(g, j, dst):
        s = lax.dot_general(
            qp[g].reshape(M, HD), kpos[cols(j, CW), :], (((1,), (1,)), ((), ())), preferred_element_type=F32
        )
        dst[...] = s
        top = ma if dst is sa else mb
        top[...] = jnp.broadcast_to(jnp.max(s, axis=1, keepdims=True), (M, 128))

    def absorb(src, j, diagonal=False):
        s = src[...]
        top = (ma if src is sa else mb)[...]
        if diagonal:
            row = lax.rem(lax.broadcasted_iota(jnp.int32, (M, CW), 0), 128)
            col = lax.broadcasted_iota(jnp.int32, (M, CW), 1)
            s = jnp.where(col <= (row // 16) * 128 + t * 16 + lax.rem(row, 16), s, NEG)
            top = jnp.max(s, axis=1, keepdims=True)
        old = m_ref[...]
        new = jnp.maximum(old, top)
        m_ref[...] = new
        factor = jnp.exp2((old - new) * SCALE)
        p = jnp.exp2(s * SCALE - jnp.tile(new * SCALE, (1, CW // 128))).astype(BF16)
        acc[...] = acc[...] * jnp.tile(factor, (1, 2)) + jnp.dot(
            p, vp[cols(j, CW), :], preferred_element_type=F32
        )

    def begin():
        m_ref[...] = jnp.full((M, 128), NEG, F32)
        acc[...] = jnp.zeros((M, 256), F32)

    def att_copy(g, da):
        at = att.at[cols(g, 128), cols(a, 512)]
        return remote(at, at, ag_s.at[g, da], ag_r.at[g, da], {"ctx": ctx_of(xh, lax.rem(a + da, 4), b)})

    def finish(g):
        for h in range(4):
            rows = slice(h * 128, h * 128 + 128)
            att[cols(g, 128), pl.ds(pl.multiple_of(a * 512 + h * 128, 128), 128)] = (
                acc[rows, :HD] / acc[rows, HD:]
            ).astype(BF16)
        for da in range(1, 4):
            att_copy(g, da).start()

    def two_groups(u, _):
        g = 2 * u
        begin()
        score(g, 0, sa)

        def even(i, _):
            score(g, 2 * i + 1, sb)
            absorb(sa, 2 * i)
            score(g, 2 * i + 2, sa)
            absorb(sb, 2 * i + 1)
            return 0

        lax.fori_loop(0, u, even, 0)
        score(g + 1, 0, sb)
        absorb(sa, g, True)
        finish(g)
        begin()

        def odd(i, _):
            score(g + 1, 2 * i + 1, sa)
            absorb(sb, 2 * i)
            score(g + 1, 2 * i + 2, sb)
            absorb(sa, 2 * i + 1)
            return 0

        lax.fori_loop(0, u, odd, 0)
        score(g + 1, g + 1, sa)
        absorb(sb, g)
        absorb(sa, g + 1, True)
        finish(g + 1)
        return 0

    lax.fori_loop(0, GROUPS // 2, two_groups, 0)

    def d_wait(kk, _):
        x_, a_, b_ = peer(kk, -1)
        at = d_recv.at[pl.ds(2 * (x_ * 16 + b_ * 4 + a_), 2)]
        remote(at, at, d_s.at[kk], d_r.at[kk], {"ctx": ctx_of(x_, a_, b_)}).wait_recv()
        return 0

    lax.fori_loop(1, N, d_wait, 0)

    def arrange_d(p, _):
        dpos[cols(p, 16), :] = d_recv[where[p]]
        return 0

    lax.fori_loop(0, 64, arrange_d, 0)
    c_w.wait()

    def project(i, _):
        for g2 in range(2):
            g = 2 * i + g2
            for da in range(1, 4):
                frm = lax.rem(a - da + 4, 4)
                at = att.at[cols(g, 128), cols(frm, 512)]
                remote(at, at, ag_s.at[g, da], ag_r.at[g, da], {"ctx": ctx_of(xh, frm, b)}).wait_recv()
        rows = cols(i, 256)
        x = jnp.dot(att[rows, :], w_v[...], preferred_element_type=F32)
        aw[pl.ds(16 * i, 16)] = x.astype(BF16).reshape(16, 16, 512)
        mg[rows, :] = ((x + dpos[rows, :].astype(F32)) * ERR).astype(BF16)
        return 0

    lax.fori_loop(0, 4, project, 0)

    def arrange_sh(blk, _):
        sh_send[blk // 2, lax.rem(blk, 2)] = aw[pos[blk]]
        return 0

    lax.fori_loop(0, 64, arrange_sh, 0)

    def sh_copy(kk):
        x_, a_, b_ = peer(kk, 1)
        to = ctx_of(x_, a_, b_)
        return remote(
            sh_send.at[to], sh_recv.at[:, cols(t, 16), cols(a, 512)], sh_s.at[kk], sh_r.at[kk], {"ctx": to}
        )

    def sh_start(kk, _):
        sh_copy(kk).start()
        return 0

    lax.fori_loop(1, N, sh_start, 0)
    sh_recv[:, cols(t, 16), cols(a, 512)] = sh_send[me]

    def wgrad(i, _):
        part = lax.dot_general(
            att[:, cols(i, 256)], mg[...], (((0,), (0,)), ((), ())), preferred_element_type=F32
        ).astype(BF16)
        for r in range(4):
            x_, mid_, low_ = i // 4, lax.rem(i, 4), r
            a_ = jnp.where(core == 0, low_, mid_)
            b_ = jnp.where(core == 0, mid_, low_)
            wg_send[x_, b_, a_] = part[r * 64 : r * 64 + 64]
        return 0

    lax.fori_loop(0, 8, wgrad, 0)

    def wa_copy(x_, db):
        to = lax.rem(b + db, 4)
        return remote(
            wg_send.at[x_, to], wa_recv.at[x_, db - 1], wa_s.at[x_, db], wa_r.at[x_, db],
            {"ctx": ctx_of(xh, a, to)},
        )

    for x_ in (xo, xh):
        for db in range(1, 4):
            wa_copy(x_, db).start()

    def wb_copy(da, far):
        to = lax.rem(a + da, 4)
        x_ = xo if far else xh
        return remote(
            wb_send.at[x_, to], wg_out_v.at[xh, :, cols(a, 512)], wb_s.at[far, da], wb_r.at[far, da],
            {"ctx": ctx_of(x_, to, b)},
        )

    for far in (1, 0):
        x_ = xo if far else xh
        for db in range(1, 4):
            frm = lax.rem(b - db + 4, 4)
            remote(
                wg_send.at[x_, frm], wa_recv.at[x_, db - 1], wa_s.at[x_, db], wa_r.at[x_, db],
                {"ctx": ctx_of(xh, a, frm)},
            ).wait_recv()
        for da in range(4):
            to = lax.rem(a + da, 4)
            total = wg_send[x_, b, to].astype(F32)
            for db in range(1, 4):
                total = total + wa_recv[x_, db - 1, to].astype(F32)
            if far == 0 and da == 0:
                wg_out_v[xh, :, cols(a, 512)] = total.astype(BF16)
            else:
                wb_send[x_, to] = total.astype(BF16)
                wb_copy(da, far).start()

    def sh_wait(kk, _):
        x_, a_, b_ = peer(kk, -1)
        at = sh_recv.at[:, cols(x_ * 4 + b_, 16), cols(a_, 512)]
        remote(sh_send.at[0], at, sh_s.at[kk], sh_r.at[kk], {"ctx": ctx_of(x_, a_, b_)}).wait_recv()
        return 0

    lax.fori_loop(1, N, sh_wait, 0)
    for far in (1, 0):
        x_ = xo if far else xh
        for da in range(4):
            if far == 0 and da == 0:
                continue
            frm = lax.rem(a - da + 4, 4)
            remote(
                wb_send.at[x_, frm], wg_out_v.at[x_, :, cols(frm, 512)], wb_s.at[far, da], wb_r.at[far, da],
                {"ctx": ctx_of(x_, frm, b)},
            ).wait_recv()

    for c in sent:
        c.wait_send()

    def drain(kk, _):
        q_copy(kk).wait_send()
        d_copy(kk).wait_send()
        sh_copy(kk).wait_send()
        return 0

    lax.fori_loop(1, N, drain, 0)

    def drain_att(g, _):
        for da in range(1, 4):
            att_copy(g, da).wait_send()
        return 0

    lax.fori_loop(0, GROUPS, drain_att, 0)
    for x_ in (xo, xh):
        for db in range(1, 4):
            wa_copy(x_, db).wait_send()
    for far in (1, 0):
        for da in range(4):
            if far or da:
                wb_copy(da, far).wait_send()


def add_up(li, sh, wg, hidden, grad):
    hidden[...] = (li[...].astype(F32) + sh[...].astype(F32)).astype(BF16)
    grad[...] = wg[0].astype(F32) + wg[1].astype(F32)


def local(query_states, key_states, value_states, layer_inputs, out_weight, teacher, teacher_map, offsets):
    pos = lax.shift_right_logical(offsets, 7)
    blk = lax.iota(jnp.int32, 64)
    home, part = blk // 2, blk % 2
    swapped = (home // 16) * 16 + (home % 4) * 4 + (home // 4) % 4
    slot = jnp.where(lax.axis_index("student") % 2 == 0, home, swapped) * 2 + part
    where = jnp.sum(jnp.where(pos[None, :] == blk[:, None], slot[None, :], 0), axis=1)
    hbm = pl.BlockSpec(memory_space=pl.ANY)
    vmem = pl.BlockSpec(memory_space=pltpu.VMEM)
    dma = pltpu.SemaphoreType.DMA
    sh, wg = pl.pallas_call(
        kernel,
        name="layer",
        out_shape=(
            jax.ShapeDtypeStruct((2, 128, 2048), BF16),
            jax.ShapeDtypeStruct((2, 64, 2048), BF16),
        ),
        in_specs=[hbm] * 7 + [pl.BlockSpec(memory_space=pltpu.SMEM)] * 2,
        out_specs=(vmem, vmem),
        scratch_shapes=[
            pltpu.VMEM((2, 128, 2048), BF16),
            pltpu.VMEM((2048, 512), BF16),
            pltpu.VMEM((256, 2048), BF16),
            pltpu.VMEM((2, 2048, 512), BF16),
            pltpu.VMEM((64, 2, 128, 128), BF16),
            pltpu.VMEM((64, 16, 512), BF16),
            pltpu.VMEM((GROUPS, 4, 128, 128), BF16),
            pltpu.VMEM((8192, 128), BF16),
            pltpu.VMEM((8192, 256), BF16),
            pltpu.VMEM((1024, 2048), BF16),
            pltpu.VMEM((2, 128, 2048), BF16),
            pltpu.VMEM((64, 16, 512), BF16),
            pltpu.VMEM((1024, 512), BF16),
            pltpu.VMEM((256, 2048), F32),
            pltpu.VMEM((128, 2048), F32),
            pltpu.VMEM((128, 2048), F32),
            pltpu.VMEM((128, 2048), BF16),
            pltpu.VMEM((128, 2048), BF16),
            pltpu.VMEM((1024, 512), BF16),
            pltpu.VMEM((64, 16, 512), BF16),
            pltpu.VMEM((32, 2, 16, 512), BF16),
            pltpu.VMEM((2, 4, 4, 64, 512), BF16),
            pltpu.VMEM((2, 3, 4, 64, 512), BF16),
            pltpu.VMEM((2, 4, 64, 512), BF16),
            pltpu.VMEM((M, CW), F32),
            pltpu.VMEM((M, CW), F32),
            pltpu.VMEM((M, 128), F32),
            pltpu.VMEM((M, 128), F32),
            pltpu.VMEM((M, 128), F32),
            pltpu.VMEM((M, 256), F32),
            dma((6,)), dma((2,)),
            dma((2, 4, 2)), dma((2, 4, 2)),
            dma((2, 4, 4)), dma((2, 4, 4)),
            dma((N,)), dma((N,)), dma((3,)), dma((3,)), dma((N,)), dma((N,)),
            dma((GROUPS, 4)), dma((GROUPS, 4)),
            dma((N,)), dma((N,)), dma((2, 4)), dma((2, 4)), dma((2, 4)), dma((2, 4)),
        ],
        compiler_params=pltpu.CompilerParams(
            collective_id=0, has_side_effects=True, vmem_limit_bytes=60 * 1024 * 1024
        ),
    )(
        query_states[0].reshape(2, 128, 2048), key_states[0].reshape(2, 128, 512), value_states[0].reshape(2, 128, 512),
        layer_inputs[0].reshape(2, 128, 2048), out_weight[0], teacher, teacher_map, pos, where,
    )
    hidden, grad = pl.pallas_call(
        add_up,
        name="add_up",
        grid=(4,),
        out_shape=(jax.ShapeDtypeStruct((256, 2048), BF16), jax.ShapeDtypeStruct((64, 2048), F32)),
        in_specs=[
            pl.BlockSpec((64, 2048), lambda i: (i, 0)),
            pl.BlockSpec((64, 2048), lambda i: (i, 0)),
            pl.BlockSpec((2, 16, 2048), lambda i: (0, i, 0)),
        ],
        out_specs=(
            pl.BlockSpec((64, 2048), lambda i: (i, 0)),
            pl.BlockSpec((16, 2048), lambda i: (i, 0)),
        ),
    )(layer_inputs[0], sh.reshape(256, 2048), wg)
    return hidden[None], grad[None]


def solution(mesh):
    return jax.shard_map(
        local,
        mesh=mesh,
        in_specs=(
            P("student", "ctx", None),
            P("student", "ctx", None),
            P("student", "ctx", None),
            P("student", "ctx", None),
            P("student", None, None),
            P("ctx", "student"),
            P("student", None),
            P(),
        ),
        out_specs=(P("student", "ctx", None), P("student", "ctx", None)),
        check_vma=False,
    )
```

```python
import math

import jax
import jax.numpy as jnp
from jax import lax
from jax.experimental import pallas as pl
from jax.experimental.pallas import tpu as pltpu
from jax.sharding import PartitionSpec as P

F32 = jnp.float32
BF16 = jnp.bfloat16
N = 32
HD = 128
SCALE = HD**-0.5 * math.log2(math.e)
ERR = 1.0 / math.sqrt(8192.0)
NEG = -1e30
GROUPS = 8
M = 512
CW = 1024
MESH = pl.DeviceIdType.MESH


def kernel(
    q, k, v, li, w, te, tm, pos, where,
    sh_recv, wg_out_v,
    li_v, w_v, te_v, tm_v, kv, q_recv, qp, kpos, vp, att, d_home, d_recv, dpos,
    tp, tx, tt, th, th_recv, mg, aw, sh_send, wg_send, wa_recv, wb_send,
    sa, sb, ma, mb, m_ref, acc,
    loc, loc_tm, s1_s, s1_r, g_s, g_r, q_s, q_r, t_s, t_r, d_s, d_r,
    ag_s, ag_r, sh_s, sh_r, wa_s, wa_r, wb_s, wb_r,
):
    stu = lax.axis_index("student")
    me = lax.axis_index("ctx")
    core = lax.rem(stu, 2)
    xlo = stu // 2
    xh = me // 16
    mid, low = lax.rem(me // 4, 4), lax.rem(me, 4)
    a = jnp.where(core == 0, low, mid)
    b = jnp.where(core == 0, mid, low)
    t = xh * 4 + b
    mine = xh * 16 + b * 4 + a

    def ctx_of(x_, a_, b_):
        return x_ * 16 + jnp.where(core == 0, b_ * 4 + a_, a_ * 4 + b_)

    def remote(src, dst, ss, rs, target):
        return pltpu.make_async_remote_copy(
            src_ref=src, dst_ref=dst, send_sem=ss, recv_sem=rs, device_id=target, device_id_type=MESH
        )

    def cols(i, width):
        return pl.ds(pl.multiple_of(i * width, width), width)

    def peer(kk, sign):
        dx, db, da = kk // 16, lax.rem(kk // 4, 4), lax.rem(kk, 4)
        x_ = lax.rem(xh + dx, 2)
        a_ = lax.rem(a + sign * da + 4, 4)
        b_ = lax.rem(b + sign * db + 4, 4)
        return x_, a_, b_

    tm_loads = [
        pltpu.make_async_copy(tm.at[:, pl.ds(512 * i, 512)], tm_v.at[i % 2], loc_tm.at[i % 2])
        for i in range(4)
    ]
    c_te = pltpu.make_async_copy(te, te_v, loc.at[0])
    c_li = pltpu.make_async_copy(li, li_v, loc.at[1])
    c_w = pltpu.make_async_copy(w.at[:, cols(a, 512)], w_v, loc.at[2])
    c_k = pltpu.make_async_copy(k.at[:, :, cols(a, HD)], kv.at[pl.ds(2 * mine, 2), 0], loc.at[3])
    c_v = pltpu.make_async_copy(v.at[:, :, cols(a, HD)], kv.at[pl.ds(2 * mine, 2), 1], loc.at[4])
    c_q = pltpu.make_async_copy(q.at[:, cols(t, 16), cols(a, 512)], q_recv.at[pl.ds(2 * mine, 2)], loc.at[5])
    for c in (c_k, c_v, c_q, c_te, tm_loads[0], tm_loads[1], c_li, c_w):
        c.start()

    barrier = pltpu.get_barrier_semaphore()

    def greet(i, _):
        pl.semaphore_signal(barrier, inc=1, device_id={"ctx": lax.rem(me + i, N)}, device_id_type=MESH)
        return 0

    lax.fori_loop(1, N, greet, 0)
    pair_core = {"student": xlo * 2 + 1 - core}
    pair_xlo = {"student": (1 - xlo) * 2 + core}
    pl.semaphore_signal(barrier, inc=1, device_id=pair_core, device_id_type=MESH)
    pl.semaphore_signal(barrier, inc=1, device_id=pair_xlo, device_id_type=MESH)
    pl.semaphore_wait(barrier, N + 1)

    xo = 1 - xh
    right, left, across = lax.rem(b + 1, 4), lax.rem(b + 3, 4), lax.rem(b + 2, 4)
    sent = []

    def first_copy(far, da, i):
        to = lax.rem(a + da, 4)
        return remote(
            (k, v)[i].at[:, :, cols(to, HD)], kv.at[pl.ds(2 * mine, 2), i], s1_s.at[far, da, i], s1_r.at[far, da, i],
            {"ctx": ctx_of(xo if far else xh, to, b)},
        )

    for far, da in ((0, 1), (1, 0), (0, 2), (1, 1), (0, 3), (1, 2), (1, 3)):
        for i in range(2):
            c = first_copy(far, da, i)
            c.start()
            sent.append(c)

    def piece(far, r, b_):
        return kv.at[pl.ds(2 * ((xo if far else xh) * 16 + b_ * 4 + lax.rem(a - r + 4, 4)), 2)]

    def hop(far, r, way, b_):
        at = piece(far, r, b_)
        return remote(
            at, at, g_s.at[far, r, way], g_r.at[far, r, way], {"ctx": ctx_of(xh, a, left if way % 2 else right)}
        )

    def pass_on(far, r):
        for i in range(2):
            if far or r:
                at = piece(far, r, b).at[:, i]
                remote(at, at, s1_s.at[far, r, i], s1_r.at[far, r, i], {"ctx": ctx_of(xh, a, right)}).wait_recv()
        for way in range(2):
            c = hop(far, r, way, b)
            c.start()
            sent.append(c)

    def relay(far, r):
        way = r % 2
        frm = right if way else left
        hop(far, r, way, frm).wait_recv()
        c = hop(far, r, 2 + way, frm)
        c.start()
        sent.append(c)

    def q_copy(kk, sign=1):
        x_, a_, b_ = peer(kk, sign)
        return remote(
            q.at[:, cols(x_ * 4 + b_, 16), cols(a_, 512)], q_recv.at[pl.ds(2 * mine, 2)], q_s.at[kk], q_r.at[kk],
            {"ctx": ctx_of(x_, a_, b_)},
        )

    def q_start(kk, _):
        q_copy(kk).start()
        return 0

    c_k.wait()
    c_v.wait()
    pass_on(0, 0)
    lax.fori_loop(1, N, q_start, 0)
    vp[:, HD:] = jnp.ones((8192, HD), BF16)
    for r in range(1, 4):
        pass_on(0, r)
    c_te.wait()
    for i in range(4):
        tm_loads[i].wait()
        tp[:, 512 * i : 512 * i + 512] = jnp.dot(te_v[...], tm_v[i % 2], preferred_element_type=F32)
        if i < 2:
            tm_loads[i + 2].start()
        pass_on(1, i)
    half = pl.ds(pl.multiple_of(core * 128, 128), 128)
    half2 = pl.ds(pl.multiple_of((1 - core) * 128, 128), 128)
    t1 = remote(tp.at[half2], tx, t_s.at[0], t_r.at[0], pair_core)
    t1.start()
    for r in range(4):
        relay(0, r)
    t1.wait()
    tp[half, :] = tp[half, :] + tx[...]
    th[...] = tp[half, :].astype(BF16)
    t2 = remote(th, th_recv, t_s.at[1], t_r.at[1], pair_xlo)
    t2.start()
    for r in range(4):
        relay(1, r)
    t2.wait()
    tp[half, :] = tp[half, :] + th_recv[...].astype(F32)
    t3 = remote(tp.at[half], tt, t_s.at[2], t_r.at[2], pair_core)
    t3.start()
    c_li.wait()
    d_home[core] = (li_v[core].astype(F32) - tp[half, :]).astype(BF16)

    c_q.wait()

    def q_wait(kk, _):
        x_, a_, b_ = peer(kk, -1)
        at = q_recv.at[pl.ds(2 * (x_ * 16 + b_ * 4 + a_), 2)]
        remote(at, at, q_s.at[kk], q_r.at[kk], {"ctx": ctx_of(x_, a_, b_)}).wait_recv()
        return 0

    lax.fori_loop(1, N, q_wait, 0)
    for far in range(2):
        for r in range(4):
            way = 1 - r % 2
            hop(far, r, way, right if way else left).wait_recv()
            hop(far, r, 2 + r % 2, across).wait_recv()
    t3.wait()
    d_home[1 - core] = (li_v[1 - core].astype(F32) - tt[...]).astype(BF16)

    def d_copy(kk):
        x_, a_, b_ = peer(kk, 1)
        return remote(
            d_home.at[:, cols(x_ * 4 + b_, 16), cols(a_, 512)], d_recv.at[pl.ds(2 * mine, 2)], d_s.at[kk], d_r.at[kk],
            {"ctx": ctx_of(x_, a_, b_)},
        )

    def d_start(kk, _):
        d_copy(kk).start()
        return 0

    lax.fori_loop(1, N, d_start, 0)
    d_recv[pl.ds(2 * mine, 2)] = d_home[:, cols(t, 16), cols(a, 512)]

    def arrange(eight, _):
        for i in range(8):
            p = eight * 8 + i
            at = where[p]
            to = pl.ds(pl.multiple_of(p * 128, 128), 128)
            kpos[to, :] = kv[at, 0]
            vp[to, :HD] = kv[at, 1]
            slab = q_recv[at]
            for h in range(4):
                qp[eight, h, 16 * i : 16 * i + 16, :] = slab[:, h * HD : h * HD + HD]
        return 0

    lax.fori_loop(0, 8, arrange, 0)

    def score(g, j, dst):
        s = lax.dot_general(
            qp[g].reshape(M, HD), kpos[cols(j, CW), :], (((1,), (1,)), ((), ())), preferred_element_type=F32
        )
        dst[...] = s
        top = ma if dst is sa else mb
        top[...] = jnp.broadcast_to(jnp.max(s, axis=1, keepdims=True), (M, 128))

    def absorb(src, j, diagonal=False):
        s = src[...]
        top = (ma if src is sa else mb)[...]
        if diagonal:
            row = lax.rem(lax.broadcasted_iota(jnp.int32, (M, CW), 0), 128)
            col = lax.broadcasted_iota(jnp.int32, (M, CW), 1)
            s = jnp.where(col <= (row // 16) * 128 + t * 16 + lax.rem(row, 16), s, NEG)
            top = jnp.max(s, axis=1, keepdims=True)
        old = m_ref[...]
        new = jnp.maximum(old, top)
        m_ref[...] = new
        factor = jnp.exp2((old - new) * SCALE)
        p = jnp.exp2(s * SCALE - jnp.tile(new * SCALE, (1, CW // 128))).astype(BF16)
        acc[...] = acc[...] * jnp.tile(factor, (1, 2)) + jnp.dot(
            p, vp[cols(j, CW), :], preferred_element_type=F32
        )

    def begin():
        m_ref[...] = jnp.full((M, 128), NEG, F32)
        acc[...] = jnp.zeros((M, 256), F32)

    def att_copy(g, da):
        at = att.at[cols(g, 128), cols(a, 512)]
        return remote(at, at, ag_s.at[g, da], ag_r.at[g, da], {"ctx": ctx_of(xh, lax.rem(a + da, 4), b)})

    def finish(g):
        for h in range(4):
            rows = slice(h * 128, h * 128 + 128)
            att[cols(g, 128), pl.ds(pl.multiple_of(a * 512 + h * 128, 128), 128)] = (
                acc[rows, :HD] / acc[rows, HD:]
            ).astype(BF16)
        for da in range(1, 4):
            att_copy(g, da).start()

    def two_groups(u, _):
        g = 2 * u
        begin()
        score(g, 0, sa)

        def even(i, _):
            score(g, 2 * i + 1, sb)
            absorb(sa, 2 * i)
            score(g, 2 * i + 2, sa)
            absorb(sb, 2 * i + 1)
            return 0

        lax.fori_loop(0, u, even, 0)
        score(g + 1, 0, sb)
        absorb(sa, g, True)
        finish(g)
        begin()

        def odd(i, _):
            score(g + 1, 2 * i + 1, sa)
            absorb(sb, 2 * i)
            score(g + 1, 2 * i + 2, sb)
            absorb(sa, 2 * i + 1)
            return 0

        lax.fori_loop(0, u, odd, 0)
        score(g + 1, g + 1, sa)
        absorb(sb, g)
        absorb(sa, g + 1, True)
        finish(g + 1)
        return 0

    lax.fori_loop(0, GROUPS // 2, two_groups, 0)

    def d_wait(kk, _):
        x_, a_, b_ = peer(kk, -1)
        at = d_recv.at[pl.ds(2 * (x_ * 16 + b_ * 4 + a_), 2)]
        remote(at, at, d_s.at[kk], d_r.at[kk], {"ctx": ctx_of(x_, a_, b_)}).wait_recv()
        return 0

    lax.fori_loop(1, N, d_wait, 0)

    def arrange_d(eight, _):
        for i in range(8):
            p = eight * 8 + i
            dpos[cols(p, 16), :] = d_recv[where[p]]
        return 0

    lax.fori_loop(0, 8, arrange_d, 0)
    c_w.wait()

    def project(i, _):
        for g2 in range(2):
            g = 2 * i + g2
            for da in range(1, 4):
                frm = lax.rem(a - da + 4, 4)
                at = att.at[cols(g, 128), cols(frm, 512)]
                remote(at, at, ag_s.at[g, da], ag_r.at[g, da], {"ctx": ctx_of(xh, frm, b)}).wait_recv()
        rows = cols(i, 256)
        x = jnp.dot(att[rows, :], w_v[...], preferred_element_type=F32)
        aw[pl.ds(16 * i, 16)] = x.astype(BF16).reshape(16, 16, 512)
        mg[rows, :] = ((x + dpos[rows, :].astype(F32)) * ERR).astype(BF16)
        return 0

    lax.fori_loop(0, 4, project, 0)

    def arrange_sh(eight, _):
        for i in range(8):
            sh_send[eight * 4 + i // 2, i % 2] = aw[pos[eight * 8 + i]]
        return 0

    lax.fori_loop(0, 8, arrange_sh, 0)

    def sh_copy(kk):
        x_, a_, b_ = peer(kk, 1)
        to = ctx_of(x_, a_, b_)
        return remote(
            sh_send.at[to], sh_recv.at[:, cols(t, 16), cols(a, 512)], sh_s.at[kk], sh_r.at[kk], {"ctx": to}
        )

    def sh_start(kk, _):
        sh_copy(kk).start()
        return 0

    lax.fori_loop(1, N, sh_start, 0)
    sh_recv[:, cols(t, 16), cols(a, 512)] = sh_send[me]

    def wgrad(i, _):
        part = lax.dot_general(
            att[:, cols(i, 256)], mg[...], (((0,), (0,)), ((), ())), preferred_element_type=F32
        ).astype(BF16)
        for r in range(4):
            x_, mid_, low_ = i // 4, lax.rem(i, 4), r
            a_ = jnp.where(core == 0, low_, mid_)
            b_ = jnp.where(core == 0, mid_, low_)
            wg_send[x_, b_, a_] = part[r * 64 : r * 64 + 64]
        return 0

    lax.fori_loop(0, 8, wgrad, 0)

    def wa_copy(x_, db):
        to = lax.rem(b + db, 4)
        return remote(
            wg_send.at[x_, to], wa_recv.at[x_, db - 1], wa_s.at[x_, db], wa_r.at[x_, db],
            {"ctx": ctx_of(xh, a, to)},
        )

    for x_ in (xo, xh):
        for db in range(1, 4):
            wa_copy(x_, db).start()

    for c in sent:
        c.wait_send()

    def drain(kk, _):
        q_copy(kk).wait_send()
        d_copy(kk).wait_send()
        return 0

    lax.fori_loop(1, N, drain, 0)

    def drain_att(g, _):
        for da in range(1, 4):
            att_copy(g, da).wait_send()
        return 0

    lax.fori_loop(0, GROUPS, drain_att, 0)
    def wb_copy(da, far):
        to = lax.rem(a + da, 4)
        x_ = xo if far else xh
        return remote(
            wb_send.at[x_, to], wg_out_v.at[xh, :, cols(a, 512)], wb_s.at[far, da], wb_r.at[far, da],
            {"ctx": ctx_of(x_, to, b)},
        )

    for far in (1, 0):
        x_ = xo if far else xh
        for db in range(1, 4):
            frm = lax.rem(b - db + 4, 4)
            remote(
                wg_send.at[x_, frm], wa_recv.at[x_, db - 1], wa_s.at[x_, db], wa_r.at[x_, db],
                {"ctx": ctx_of(xh, a, frm)},
            ).wait_recv()
        for da in range(4):
            to = lax.rem(a + da, 4)
            total = wg_send[x_, b, to].astype(F32)
            for db in range(1, 4):
                total = total + wa_recv[x_, db - 1, to].astype(F32)
            if far == 0 and da == 0:
                wg_out_v[xh, :, cols(a, 512)] = total.astype(BF16)
            else:
                wb_send[x_, to] = total.astype(BF16)
                wb_copy(da, far).start()

    def sh_wait(kk, _):
        x_, a_, b_ = peer(kk, -1)
        at = sh_recv.at[:, cols(x_ * 4 + b_, 16), cols(a_, 512)]
        remote(sh_send.at[0], at, sh_s.at[kk], sh_r.at[kk], {"ctx": ctx_of(x_, a_, b_)}).wait_recv()
        return 0

    lax.fori_loop(1, N, sh_wait, 0)

    def sh_drain(kk, _):
        sh_copy(kk).wait_send()
        return 0

    lax.fori_loop(1, N, sh_drain, 0)
    for far in (1, 0):
        x_ = xo if far else xh
        for da in range(4):
            if far == 0 and da == 0:
                continue
            frm = lax.rem(a - da + 4, 4)
            remote(
                wb_send.at[x_, frm], wg_out_v.at[x_, :, cols(frm, 512)], wb_s.at[far, da], wb_r.at[far, da],
                {"ctx": ctx_of(x_, frm, b)},
            ).wait_recv()

    for x_ in (xo, xh):
        for db in range(1, 4):
            wa_copy(x_, db).wait_send()
    for far in (1, 0):
        for da in range(4):
            if far or da:
                wb_copy(da, far).wait_send()


def add_up(li, sh, wg, hidden, grad):
    hidden[...] = (li[...].astype(F32) + sh[...].astype(F32)).astype(BF16)
    grad[...] = wg[0].astype(F32) + wg[1].astype(F32)


def local(query_states, key_states, value_states, layer_inputs, out_weight, teacher, teacher_map, offsets):
    pos = lax.shift_right_logical(offsets, 7)
    blk = lax.iota(jnp.int32, 64)
    home, part = blk // 2, blk % 2
    swapped = (home // 16) * 16 + (home % 4) * 4 + (home // 4) % 4
    slot = jnp.where(lax.axis_index("student") % 2 == 0, home, swapped) * 2 + part
    where = jnp.sum(jnp.where(pos[None, :] == blk[:, None], slot[None, :], 0), axis=1)
    hbm = pl.BlockSpec(memory_space=pl.ANY)
    vmem = pl.BlockSpec(memory_space=pltpu.VMEM)
    dma = pltpu.SemaphoreType.DMA
    sh, wg = pl.pallas_call(
        kernel,
        name="layer",
        out_shape=(
            jax.ShapeDtypeStruct((2, 128, 2048), BF16),
            jax.ShapeDtypeStruct((2, 64, 2048), BF16),
        ),
        in_specs=[hbm] * 7 + [pl.BlockSpec(memory_space=pltpu.SMEM)] * 2,
        out_specs=(vmem, vmem),
        scratch_shapes=[
            pltpu.VMEM((2, 128, 2048), BF16),
            pltpu.VMEM((2048, 512), BF16),
            pltpu.VMEM((256, 2048), BF16),
            pltpu.VMEM((2, 2048, 512), BF16),
            pltpu.VMEM((64, 2, 128, 128), BF16),
            pltpu.VMEM((64, 16, 512), BF16),
            pltpu.VMEM((GROUPS, 4, 128, 128), BF16),
            pltpu.VMEM((8192, 128), BF16),
            pltpu.VMEM((8192, 256), BF16),
            pltpu.VMEM((1024, 2048), BF16),
            pltpu.VMEM((2, 128, 2048), BF16),
            pltpu.VMEM((64, 16, 512), BF16),
            pltpu.VMEM((1024, 512), BF16),
            pltpu.VMEM((256, 2048), F32),
            pltpu.VMEM((128, 2048), F32),
            pltpu.VMEM((128, 2048), F32),
            pltpu.VMEM((128, 2048), BF16),
            pltpu.VMEM((128, 2048), BF16),
            pltpu.VMEM((1024, 512), BF16),
            pltpu.VMEM((64, 16, 512), BF16),
            pltpu.VMEM((32, 2, 16, 512), BF16),
            pltpu.VMEM((2, 4, 4, 64, 512), BF16),
            pltpu.VMEM((2, 3, 4, 64, 512), BF16),
            pltpu.VMEM((2, 4, 64, 512), BF16),
            pltpu.VMEM((M, CW), F32),
            pltpu.VMEM((M, CW), F32),
            pltpu.VMEM((M, 128), F32),
            pltpu.VMEM((M, 128), F32),
            pltpu.VMEM((M, 128), F32),
            pltpu.VMEM((M, 256), F32),
            dma((6,)), dma((2,)),
            dma((2, 4, 2)), dma((2, 4, 2)),
            dma((2, 4, 4)), dma((2, 4, 4)),
            dma((N,)), dma((N,)), dma((3,)), dma((3,)), dma((N,)), dma((N,)),
            dma((GROUPS, 4)), dma((GROUPS, 4)),
            dma((N,)), dma((N,)), dma((2, 4)), dma((2, 4)), dma((2, 4)), dma((2, 4)),
        ],
        compiler_params=pltpu.CompilerParams(
            collective_id=0, has_side_effects=True, vmem_limit_bytes=60 * 1024 * 1024
        ),
    )(
        query_states[0].reshape(2, 128, 2048), key_states[0].reshape(2, 128, 512), value_states[0].reshape(2, 128, 512),
        layer_inputs[0].reshape(2, 128, 2048), out_weight[0], teacher, teacher_map, pos, where,
    )
    hidden, grad = pl.pallas_call(
        add_up,
        name="add_up",
        grid=(4,),
        out_shape=(jax.ShapeDtypeStruct((256, 2048), BF16), jax.ShapeDtypeStruct((64, 2048), F32)),
        in_specs=[
            pl.BlockSpec((64, 2048), lambda i: (i, 0)),
            pl.BlockSpec((64, 2048), lambda i: (i, 0)),
            pl.BlockSpec((2, 16, 2048), lambda i: (0, i, 0)),
        ],
        out_specs=(
            pl.BlockSpec((64, 2048), lambda i: (i, 0)),
            pl.BlockSpec((16, 2048), lambda i: (i, 0)),
        ),
    )(layer_inputs[0], sh.reshape(256, 2048), wg)
    return hidden[None], grad[None]


def solution(mesh):
    return jax.shard_map(
        local,
        mesh=mesh,
        in_specs=(
            P("student", "ctx", None),
            P("student", "ctx", None),
            P("student", "ctx", None),
            P("student", "ctx", None),
            P("student", None, None),
            P("ctx", "student"),
            P("student", None),
            P(),
        ),
        out_specs=(P("student", "ctx", None), P("student", "ctx", None)),
        check_vma=False,
    )
```

```python
import math

import jax
import jax.numpy as jnp
from jax import lax
from jax.experimental import pallas as pl
from jax.experimental.pallas import tpu as pltpu
from jax.sharding import PartitionSpec as P

F32 = jnp.float32
BF16 = jnp.bfloat16
N = 32
HD = 128
SCALE = HD**-0.5 * math.log2(math.e)
ERR = 1.0 / math.sqrt(8192.0)
NEG = -1e30
GROUPS = 8
M = 512
CW = 1024
MESH = pl.DeviceIdType.MESH


def kernel(
    q, k, v, li, w, te, tm, pos, where,
    sh_recv, wg_out_v,
    li_v, w_v, te_v, tm_v, kv, q_recv, qp, kpos, vp, att, d_home, d_recv, dpos,
    tp, tx, tt, th, th_recv, mg, aw, sh_send, wg_send, wa_recv, wb_send,
    sa, sb, ma, mb, m_ref, acc,
    loc, loc_tm, s1_s, s1_r, g_s, g_r, q_s, q_r, t_s, t_r, d_s, d_r,
    ag_s, ag_r, sh_s, sh_r, wa_s, wa_r, wb_s, wb_r,
):
    stu = lax.axis_index("student")
    me = lax.axis_index("ctx")
    core = lax.rem(stu, 2)
    xlo = stu // 2
    xh = me // 16
    mid, low = lax.rem(me // 4, 4), lax.rem(me, 4)
    a = jnp.where(core == 0, low, mid)
    b = jnp.where(core == 0, mid, low)
    t = xh * 4 + b
    mine = xh * 16 + b * 4 + a

    def ctx_of(x_, a_, b_):
        return x_ * 16 + jnp.where(core == 0, b_ * 4 + a_, a_ * 4 + b_)

    def remote(src, dst, ss, rs, target):
        return pltpu.make_async_remote_copy(
            src_ref=src, dst_ref=dst, send_sem=ss, recv_sem=rs, device_id=target, device_id_type=MESH
        )

    def cols(i, width):
        return pl.ds(pl.multiple_of(i * width, width), width)

    def peer(kk, sign):
        dx, db, da = kk // 16, lax.rem(kk // 4, 4), lax.rem(kk, 4)
        x_ = lax.rem(xh + dx, 2)
        a_ = lax.rem(a + sign * da + 4, 4)
        b_ = lax.rem(b + sign * db + 4, 4)
        return x_, a_, b_

    tm_loads = [
        pltpu.make_async_copy(tm.at[:, pl.ds(512 * i, 512)], tm_v.at[i % 2], loc_tm.at[i % 2])
        for i in range(4)
    ]
    c_te = pltpu.make_async_copy(te, te_v, loc.at[0])
    c_li = pltpu.make_async_copy(li, li_v, loc.at[1])
    c_w = pltpu.make_async_copy(w.at[:, cols(a, 512)], w_v, loc.at[2])
    c_k = pltpu.make_async_copy(k.at[:, :, cols(a, HD)], kv.at[pl.ds(2 * mine, 2), 0], loc.at[3])
    c_v = pltpu.make_async_copy(v.at[:, :, cols(a, HD)], kv.at[pl.ds(2 * mine, 2), 1], loc.at[4])
    c_q = pltpu.make_async_copy(q.at[:, cols(t, 16), cols(a, 512)], q_recv.at[pl.ds(2 * mine, 2)], loc.at[5])
    for c in (c_k, c_v, c_q, c_te, tm_loads[0], tm_loads[1], c_li, c_w):
        c.start()

    barrier = pltpu.get_barrier_semaphore()

    def greet(i, _):
        pl.semaphore_signal(barrier, inc=1, device_id={"ctx": lax.rem(me + i, N)}, device_id_type=MESH)
        return 0

    lax.fori_loop(1, N, greet, 0)
    pair_core = {"student": xlo * 2 + 1 - core}
    pair_xlo = {"student": (1 - xlo) * 2 + core}
    pl.semaphore_signal(barrier, inc=1, device_id=pair_core, device_id_type=MESH)
    pl.semaphore_signal(barrier, inc=1, device_id=pair_xlo, device_id_type=MESH)
    pl.semaphore_wait(barrier, N + 1)

    xo = 1 - xh
    right, left, across = lax.rem(b + 1, 4), lax.rem(b + 3, 4), lax.rem(b + 2, 4)
    sent = []

    def first_copy(far, da, i):
        to = lax.rem(a + da, 4)
        return remote(
            (k, v)[i].at[:, :, cols(to, HD)], kv.at[pl.ds(2 * mine, 2), i], s1_s.at[far, da, i], s1_r.at[far, da, i],
            {"ctx": ctx_of(xo if far else xh, to, b)},
        )

    for far, da in ((0, 1), (1, 0), (0, 2), (1, 1), (0, 3), (1, 2), (1, 3)):
        for i in range(2):
            c = first_copy(far, da, i)
            c.start()
            sent.append(c)

    def piece(far, r, b_):
        return kv.at[pl.ds(2 * ((xo if far else xh) * 16 + b_ * 4 + lax.rem(a - r + 4, 4)), 2)]

    def hop(far, r, way, b_):
        at = piece(far, r, b_)
        return remote(
            at, at, g_s.at[far, r, way], g_r.at[far, r, way], {"ctx": ctx_of(xh, a, left if way % 2 else right)}
        )

    def pass_on(far, r):
        for i in range(2):
            if far or r:
                at = piece(far, r, b).at[:, i]
                remote(at, at, s1_s.at[far, r, i], s1_r.at[far, r, i], {"ctx": ctx_of(xh, a, right)}).wait_recv()
        for way in range(2):
            c = hop(far, r, way, b)
            c.start()
            sent.append(c)

    def relay(far, r):
        way = r % 2
        frm = right if way else left
        hop(far, r, way, frm).wait_recv()
        c = hop(far, r, 2 + way, frm)
        c.start()
        sent.append(c)

    def q_copy(kk, sign=1):
        x_, a_, b_ = peer(kk, sign)
        return remote(
            q.at[:, cols(x_ * 4 + b_, 16), cols(a_, 512)], q_recv.at[pl.ds(2 * mine, 2)], q_s.at[kk], q_r.at[kk],
            {"ctx": ctx_of(x_, a_, b_)},
        )

    def q_start(kk, _):
        q_copy(kk).start()
        return 0

    c_k.wait()
    c_v.wait()
    pass_on(0, 0)
    lax.fori_loop(1, N, q_start, 0)
    vp[:, HD:] = jnp.ones((8192, HD), BF16)
    for r in range(1, 4):
        pass_on(0, r)
    c_te.wait()
    for i in range(4):
        tm_loads[i].wait()
        tp[:, 512 * i : 512 * i + 512] = jnp.dot(te_v[...], tm_v[i % 2], preferred_element_type=F32)
        if i < 2:
            tm_loads[i + 2].start()
        pass_on(1, i)
    half = pl.ds(pl.multiple_of(core * 128, 128), 128)
    half2 = pl.ds(pl.multiple_of((1 - core) * 128, 128), 128)
    t1 = remote(tp.at[half2], tx, t_s.at[0], t_r.at[0], pair_core)
    t1.start()
    for r in range(4):
        relay(0, r)
    t1.wait()
    tp[half, :] = tp[half, :] + tx[...]
    th[...] = tp[half, :].astype(BF16)
    t2 = remote(th, th_recv, t_s.at[1], t_r.at[1], pair_xlo)
    t2.start()
    for r in range(4):
        relay(1, r)
    t2.wait()
    tp[half, :] = tp[half, :] + th_recv[...].astype(F32)
    t3 = remote(tp.at[half], tt, t_s.at[2], t_r.at[2], pair_core)
    t3.start()
    c_li.wait()
    d_home[core] = (li_v[core].astype(F32) - tp[half, :]).astype(BF16)

    c_q.wait()

    def q_wait(kk, _):
        x_, a_, b_ = peer(kk, -1)
        at = q_recv.at[pl.ds(2 * (x_ * 16 + b_ * 4 + a_), 2)]
        remote(at, at, q_s.at[kk], q_r.at[kk], {"ctx": ctx_of(x_, a_, b_)}).wait_recv()
        return 0

    lax.fori_loop(1, N, q_wait, 0)
    for far in range(2):
        for r in range(4):
            way = 1 - r % 2
            hop(far, r, way, right if way else left).wait_recv()
            hop(far, r, 2 + r % 2, across).wait_recv()
    t3.wait()
    d_home[1 - core] = (li_v[1 - core].astype(F32) - tt[...]).astype(BF16)

    def d_copy(kk):
        x_, a_, b_ = peer(kk, 1)
        return remote(
            d_home.at[:, cols(x_ * 4 + b_, 16), cols(a_, 512)], d_recv.at[pl.ds(2 * mine, 2)], d_s.at[kk], d_r.at[kk],
            {"ctx": ctx_of(x_, a_, b_)},
        )

    def d_start(kk, _):
        d_copy(kk).start()
        return 0

    lax.fori_loop(1, N, d_start, 0)
    d_recv[pl.ds(2 * mine, 2)] = d_home[:, cols(t, 16), cols(a, 512)]

    def arrange(eight, _):
        for i in range(8):
            p = eight * 8 + i
            at = where[p]
            to = pl.ds(pl.multiple_of(p * 128, 128), 128)
            kpos[to, :] = kv[at, 0]
            vp[to, :HD] = kv[at, 1]
            slab = q_recv[at]
            for h in range(4):
                qp[eight, i // 4 * 4 + h, 16 * (i % 4) : 16 * (i % 4) + 16, :] = slab[:, h * HD : h * HD + HD]
        return 0

    lax.fori_loop(0, 8, arrange, 0)

    def score(g, j, dst):
        s = lax.dot_general(
            qp[g].reshape(M, HD), kpos[cols(j, CW), :], (((1,), (1,)), ((), ())), preferred_element_type=F32
        )
        dst[...] = s
        top = ma if dst is sa else mb
        top[...] = jnp.broadcast_to(jnp.max(s, axis=1, keepdims=True), (M, 128))

    def update(first, s, top, keys):
        rows = pl.ds(first, M - first)
        old = m_ref[rows, :]
        new = jnp.maximum(old, top)
        m_ref[rows, :] = new
        factor = jnp.exp2((old - new) * SCALE)
        p = jnp.exp2(s * SCALE - jnp.tile(new * SCALE, (1, s.shape[1] // 128))).astype(BF16)
        acc[rows, :] = acc[rows, :] * jnp.tile(factor, (1, 2)) + jnp.dot(
            p, vp[keys, :], preferred_element_type=F32
        )

    def absorb(src, j, diagonal=False):
        if not diagonal:
            update(0, src[...], (ma if src is sa else mb)[...], cols(j, CW))
            return
        row = lax.broadcasted_iota(jnp.int32, (256, 512), 0)
        col = lax.broadcasted_iota(jnp.int32, (256, 512), 1)
        ok = col <= (lax.rem(row, 64) // 16) * 128 + t * 16 + lax.rem(row, 16)
        s = jnp.concatenate([jnp.where(ok, src[:256, :512], NEG), src[256:, :512]], axis=0)
        update(0, s, jnp.max(s, axis=1, keepdims=True), cols(2 * j, 512))
        s = jnp.where(ok, src[256:, 512:], NEG)
        update(256, s, jnp.max(s, axis=1, keepdims=True), cols(2 * j + 1, 512))

    def begin():
        m_ref[...] = jnp.full((M, 128), NEG, F32)
        acc[...] = jnp.zeros((M, 256), F32)

    def att_copy(g, da):
        at = att.at[cols(g, 128), cols(a, 512)]
        return remote(at, at, ag_s.at[g, da], ag_r.at[g, da], {"ctx": ctx_of(xh, lax.rem(a + da, 4), b)})

    def finish(g):
        for i in range(8):
            rows = slice(i * 64, i * 64 + 64)
            to = pl.ds(pl.multiple_of(g * 128 + i // 4 * 64, 64), 64)
            att[to, pl.ds(pl.multiple_of(a * 512 + i % 4 * 128, 128), 128)] = (
                acc[rows, :HD] / acc[rows, HD:]
            ).astype(BF16)
        for da in range(1, 4):
            att_copy(g, da).start()

    def two_groups(u, _):
        g = 2 * u
        begin()
        score(g, 0, sa)

        def even(i, _):
            score(g, 2 * i + 1, sb)
            absorb(sa, 2 * i)
            score(g, 2 * i + 2, sa)
            absorb(sb, 2 * i + 1)
            return 0

        lax.fori_loop(0, u, even, 0)
        score(g + 1, 0, sb)
        absorb(sa, g, True)
        finish(g)
        begin()

        def odd(i, _):
            score(g + 1, 2 * i + 1, sa)
            absorb(sb, 2 * i)
            score(g + 1, 2 * i + 2, sb)
            absorb(sa, 2 * i + 1)
            return 0

        lax.fori_loop(0, u, odd, 0)
        score(g + 1, g + 1, sa)
        absorb(sb, g)
        absorb(sa, g + 1, True)
        finish(g + 1)
        return 0

    lax.fori_loop(0, GROUPS // 2, two_groups, 0)

    def d_wait(kk, _):
        x_, a_, b_ = peer(kk, -1)
        at = d_recv.at[pl.ds(2 * (x_ * 16 + b_ * 4 + a_), 2)]
        remote(at, at, d_s.at[kk], d_r.at[kk], {"ctx": ctx_of(x_, a_, b_)}).wait_recv()
        return 0

    lax.fori_loop(1, N, d_wait, 0)

    def arrange_d(eight, _):
        for i in range(8):
            p = eight * 8 + i
            dpos[cols(p, 16), :] = d_recv[where[p]]
        return 0

    lax.fori_loop(0, 8, arrange_d, 0)
    c_w.wait()

    def project(i, _):
        for g2 in range(2):
            g = 2 * i + g2
            for da in range(1, 4):
                frm = lax.rem(a - da + 4, 4)
                at = att.at[cols(g, 128), cols(frm, 512)]
                remote(at, at, ag_s.at[g, da], ag_r.at[g, da], {"ctx": ctx_of(xh, frm, b)}).wait_recv()
        rows = cols(i, 256)
        x = jnp.dot(att[rows, :], w_v[...], preferred_element_type=F32)
        aw[pl.ds(16 * i, 16)] = x.astype(BF16).reshape(16, 16, 512)
        mg[rows, :] = ((x + dpos[rows, :].astype(F32)) * ERR).astype(BF16)
        return 0

    lax.fori_loop(0, 4, project, 0)

    def arrange_sh(eight, _):
        for i in range(8):
            sh_send[eight * 4 + i // 2, i % 2] = aw[pos[eight * 8 + i]]
        return 0

    lax.fori_loop(0, 8, arrange_sh, 0)

    def sh_copy(kk):
        x_, a_, b_ = peer(kk, 1)
        to = ctx_of(x_, a_, b_)
        return remote(
            sh_send.at[to], sh_recv.at[:, cols(t, 16), cols(a, 512)], sh_s.at[kk], sh_r.at[kk], {"ctx": to}
        )

    def sh_start(kk, _):
        sh_copy(kk).start()
        return 0

    lax.fori_loop(1, N, sh_start, 0)
    sh_recv[:, cols(t, 16), cols(a, 512)] = sh_send[me]

    def wgrad(i, _):
        part = lax.dot_general(
            att[:, cols(i, 256)], mg[...], (((0,), (0,)), ((), ())), preferred_element_type=F32
        ).astype(BF16)
        for r in range(4):
            x_, mid_, low_ = i // 4, lax.rem(i, 4), r
            a_ = jnp.where(core == 0, low_, mid_)
            b_ = jnp.where(core == 0, mid_, low_)
            wg_send[x_, b_, a_] = part[r * 64 : r * 64 + 64]
        return 0

    lax.fori_loop(0, 8, wgrad, 0)

    def wa_copy(x_, db):
        to = lax.rem(b + db, 4)
        return remote(
            wg_send.at[x_, to], wa_recv.at[x_, db - 1], wa_s.at[x_, db], wa_r.at[x_, db],
            {"ctx": ctx_of(xh, a, to)},
        )

    for x_ in (xo, xh):
        for db in range(1, 4):
            wa_copy(x_, db).start()

    for c in sent:
        c.wait_send()

    def drain(kk, _):
        q_copy(kk).wait_send()
        d_copy(kk).wait_send()
        return 0

    lax.fori_loop(1, N, drain, 0)

    def drain_att(g, _):
        for da in range(1, 4):
            att_copy(g, da).wait_send()
        return 0

    lax.fori_loop(0, GROUPS, drain_att, 0)
    def wb_copy(da, far):
        to = lax.rem(a + da, 4)
        x_ = xo if far else xh
        return remote(
            wb_send.at[x_, to], wg_out_v.at[xh, :, cols(a, 512)], wb_s.at[far, da], wb_r.at[far, da],
            {"ctx": ctx_of(x_, to, b)},
        )

    for far in (1, 0):
        x_ = xo if far else xh
        for db in range(1, 4):
            frm = lax.rem(b - db + 4, 4)
            remote(
                wg_send.at[x_, frm], wa_recv.at[x_, db - 1], wa_s.at[x_, db], wa_r.at[x_, db],
                {"ctx": ctx_of(xh, a, frm)},
            ).wait_recv()
        for da in range(4):
            to = lax.rem(a + da, 4)
            total = wg_send[x_, b, to].astype(F32)
            for db in range(1, 4):
                total = total + wa_recv[x_, db - 1, to].astype(F32)
            if far == 0 and da == 0:
                wg_out_v[xh, :, cols(a, 512)] = total.astype(BF16)
            else:
                wb_send[x_, to] = total.astype(BF16)
                wb_copy(da, far).start()

    def sh_wait(kk, _):
        x_, a_, b_ = peer(kk, -1)
        at = sh_recv.at[:, cols(x_ * 4 + b_, 16), cols(a_, 512)]
        remote(sh_send.at[0], at, sh_s.at[kk], sh_r.at[kk], {"ctx": ctx_of(x_, a_, b_)}).wait_recv()
        return 0

    lax.fori_loop(1, N, sh_wait, 0)

    def sh_drain(kk, _):
        sh_copy(kk).wait_send()
        return 0

    lax.fori_loop(1, N, sh_drain, 0)
    for far in (1, 0):
        x_ = xo if far else xh
        for da in range(4):
            if far == 0 and da == 0:
                continue
            frm = lax.rem(a - da + 4, 4)
            remote(
                wb_send.at[x_, frm], wg_out_v.at[x_, :, cols(frm, 512)], wb_s.at[far, da], wb_r.at[far, da],
                {"ctx": ctx_of(x_, frm, b)},
            ).wait_recv()

    for x_ in (xo, xh):
        for db in range(1, 4):
            wa_copy(x_, db).wait_send()
    for far in (1, 0):
        for da in range(4):
            if far or da:
                wb_copy(da, far).wait_send()


def add_up(li, sh, wg, hidden, grad):
    hidden[...] = (li[...].astype(F32) + sh[...].astype(F32)).astype(BF16)
    grad[...] = wg[0].astype(F32) + wg[1].astype(F32)


def local(query_states, key_states, value_states, layer_inputs, out_weight, teacher, teacher_map, offsets):
    pos = lax.shift_right_logical(offsets, 7)
    blk = lax.iota(jnp.int32, 64)
    home, part = blk // 2, blk % 2
    swapped = (home // 16) * 16 + (home % 4) * 4 + (home // 4) % 4
    slot = jnp.where(lax.axis_index("student") % 2 == 0, home, swapped) * 2 + part
    where = jnp.sum(jnp.where(pos[None, :] == blk[:, None], slot[None, :], 0), axis=1)
    hbm = pl.BlockSpec(memory_space=pl.ANY)
    vmem = pl.BlockSpec(memory_space=pltpu.VMEM)
    dma = pltpu.SemaphoreType.DMA
    sh, wg = pl.pallas_call(
        kernel,
        name="layer",
        out_shape=(
            jax.ShapeDtypeStruct((2, 128, 2048), BF16),
            jax.ShapeDtypeStruct((2, 64, 2048), BF16),
        ),
        in_specs=[hbm] * 7 + [pl.BlockSpec(memory_space=pltpu.SMEM)] * 2,
        out_specs=(vmem, vmem),
        scratch_shapes=[
            pltpu.VMEM((2, 128, 2048), BF16),
            pltpu.VMEM((2048, 512), BF16),
            pltpu.VMEM((256, 2048), BF16),
            pltpu.VMEM((2, 2048, 512), BF16),
            pltpu.VMEM((64, 2, 128, 128), BF16),
            pltpu.VMEM((64, 16, 512), BF16),
            pltpu.VMEM((GROUPS, 8, 64, 128), BF16),
            pltpu.VMEM((8192, 128), BF16),
            pltpu.VMEM((8192, 256), BF16),
            pltpu.VMEM((1024, 2048), BF16),
            pltpu.VMEM((2, 128, 2048), BF16),
            pltpu.VMEM((64, 16, 512), BF16),
            pltpu.VMEM((1024, 512), BF16),
            pltpu.VMEM((256, 2048), F32),
            pltpu.VMEM((128, 2048), F32),
            pltpu.VMEM((128, 2048), F32),
            pltpu.VMEM((128, 2048), BF16),
            pltpu.VMEM((128, 2048), BF16),
            pltpu.VMEM((1024, 512), BF16),
            pltpu.VMEM((64, 16, 512), BF16),
            pltpu.VMEM((32, 2, 16, 512), BF16),
            pltpu.VMEM((2, 4, 4, 64, 512), BF16),
            pltpu.VMEM((2, 3, 4, 64, 512), BF16),
            pltpu.VMEM((2, 4, 64, 512), BF16),
            pltpu.VMEM((M, CW), F32),
            pltpu.VMEM((M, CW), F32),
            pltpu.VMEM((M, 128), F32),
            pltpu.VMEM((M, 128), F32),
            pltpu.VMEM((M, 128), F32),
            pltpu.VMEM((M, 256), F32),
            dma((6,)), dma((2,)),
            dma((2, 4, 2)), dma((2, 4, 2)),
            dma((2, 4, 4)), dma((2, 4, 4)),
            dma((N,)), dma((N,)), dma((3,)), dma((3,)), dma((N,)), dma((N,)),
            dma((GROUPS, 4)), dma((GROUPS, 4)),
            dma((N,)), dma((N,)), dma((2, 4)), dma((2, 4)), dma((2, 4)), dma((2, 4)),
        ],
        compiler_params=pltpu.CompilerParams(
            collective_id=0, has_side_effects=True, vmem_limit_bytes=60 * 1024 * 1024
        ),
    )(
        query_states[0].reshape(2, 128, 2048), key_states[0].reshape(2, 128, 512), value_states[0].reshape(2, 128, 512),
        layer_inputs[0].reshape(2, 128, 2048), out_weight[0], teacher, teacher_map, pos, where,
    )
    hidden, grad = pl.pallas_call(
        add_up,
        name="add_up",
        grid=(4,),
        out_shape=(jax.ShapeDtypeStruct((256, 2048), BF16), jax.ShapeDtypeStruct((64, 2048), F32)),
        in_specs=[
            pl.BlockSpec((64, 2048), lambda i: (i, 0)),
            pl.BlockSpec((64, 2048), lambda i: (i, 0)),
            pl.BlockSpec((2, 16, 2048), lambda i: (0, i, 0)),
        ],
        out_specs=(
            pl.BlockSpec((64, 2048), lambda i: (i, 0)),
            pl.BlockSpec((16, 2048), lambda i: (i, 0)),
        ),
    )(layer_inputs[0], sh.reshape(256, 2048), wg)
    return hidden[None], grad[None]


def solution(mesh):
    return jax.shard_map(
        local,
        mesh=mesh,
        in_specs=(
            P("student", "ctx", None),
            P("student", "ctx", None),
            P("student", "ctx", None),
            P("student", "ctx", None),
            P("student", None, None),
            P("ctx", "student"),
            P("student", None),
            P(),
        ),
        out_specs=(P("student", "ctx", None), P("student", "ctx", None)),
        check_vma=False,
    )
```
